256 devices in a mesh: dp: 4 (over z_hi, core), tensor: 64 (over y, x, z_lo).
Axes of the slice: x: 4, y: 4, z: 8 (z_hi: 2, z_lo: 4; z = z_hi * 4 + z_lo), core: 2. Of those that a mesh axis runs over, the one named last changes fastest.
Arguments:
- hidden: bfloat16 [1024, 28672], P('dp', 'tensor'), may hold values from -6 to 6
- weight: bfloat16 [28672, 8192], P('tensor'), may hold values from -0.09375 to 0.09375
- factors: bfloat16 [6, 448, 64, 64], P(None, 'tensor'), may hold values from -0.29882812 to 0.29882812
- cotangent: bfloat16 [1024, 8192], P('dp', 'tensor'), may hold values from -6 to 6
Outputs:
- projected: bfloat16 [1024, 8192], P('dp', 'tensor')
- hidden_grad: bfloat16 [1024, 28672], P('dp', 'tensor')
- factor_grad: float32 [6, 448, 64, 64], P(None, 'tensor')
The draws below stay inside these ranges and needn't reach their ends.
All inputs are finite; a program needn't handle non-finite values.
Results may differ from the reference program's by a relative error of at most 0.02.
Values may be sent and summed in bfloat16 or wider, within the bound.
A program may use at most 128 MiB of HBM per device.

```python
import jax
import jax.numpy as jnp

D = 8192
FF = 28672
BLK = 64
SECTIONS = 6
QB = 64
LANES = 7
NB = 448
TOKENS = 1024


def spiked(entries, key, source, target, blocks, factor):
    owner, partner = [(jnp.arange(entries.shape[position]) // (entries.shape[position] // blocks)).reshape([-1 if axis == position else 1 for axis in range(entries.ndim)]) for position in (source, target)]
    chosen = jax.random.permutation(key, blocks)[partner]
    strong = (owner == chosen) | (owner == (partner + blocks // 2) % blocks)
    return jnp.where(strong, factor * entries, entries)


def levels(rng, dims, shards, low, top_value):
    def one(position, shards_of):
        steps = jax.random.uniform(jax.random.fold_in(jax.random.fold_in(rng, 6), position), (shards_of,), jnp.float32, low / len(shards), top_value / len(shards))
        return jnp.repeat(jnp.exp(steps), dims[position] // shards_of).reshape((-1,) + (1,) * (len(dims) - position - 1))

    loudness = one(*shards[0])
    for cut in shards[1:]:
        loudness = loudness * one(*cut)
    return loudness


def bell_draw(rng, shape, scale, reach, shards=(), kind=jnp.bfloat16):
    array = scale * jax.random.normal(rng, shape, jnp.float32)
    if shards:
        array = array * levels(rng, shape, shards, -0.22, 0.18)
    return jnp.clip(array, -reach, reach).astype(kind)


def gaussian_with(own_key, dims, scale, bound, pieces, heavy, kind=jnp.bfloat16):
    entries = scale * jax.random.normal(own_key, dims, jnp.float32)
    if pieces:
        entries = entries * levels(own_key, dims, pieces, -0.22, 0.18)
    return jnp.clip(spiked(entries, jax.random.fold_in(own_key, 3), *heavy), -bound, bound).astype(kind)


def setup_inputs(seed: int = 0) -> dict:
    streams_of = jax.random.split(jax.random.key(seed), 5)
    return {
        "hidden": bell_draw(streams_of[0], (TOKENS, FF), 1.0, 6.0, ((0, 4), (1, 64))),
        "weight": gaussian_with(streams_of[1], (FF, D), FF ** -0.5, 0.09375, ((0, 64),), (0, 1, 64, 4.0)),
        "factors": bell_draw(streams_of[2], (SECTIONS, NB, BLK, BLK), 0.05, 0.29882812, ((1, 64),)),
        "cotangent": bell_draw(streams_of[3], (TOKENS, D), 1.0, 6.0, ((0, 4), (1, 64))),
    }


def pair_layout(values, section_no):
    outer_n = QB >> (section_no + 1)
    inner_n = 1 << section_no
    half_width = BLK // 2
    return values.reshape(values.shape[0], outer_n, 2, inner_n, LANES, 2, half_width).astype(jnp.float32)


def factor_layout(factor_one, section_no):
    outer_n = QB >> (section_no + 1)
    inner_n = 1 << section_no
    half_width = BLK // 2
    return factor_one.reshape(outer_n, 2, inner_n, LANES, BLK, 2, half_width).astype(jnp.float32)


def section_inputs(current, section_no):
    arranged = pair_layout(current, section_no)
    return arranged, jnp.concatenate([arranged[:, :, 0], arranged[:, :, 1]], axis=-1)


def section_forward(current, factor_one, section_no):
    arranged, mixed_in = section_inputs(current, section_no)
    fac_r = factor_layout(factor_one, section_no)
    mix_term = jnp.einsum('tacjhm,abcjmhk->tabcjhk', mixed_in, fac_r)
    return (arranged + mix_term).astype(jnp.bfloat16).reshape(current.shape)


def section_backward(current, factor_one, grad_next, section_no):
    arranged, mixed_in = section_inputs(current, section_no)
    fac_r = factor_layout(factor_one, section_no)
    grad_r = pair_layout(grad_next, section_no)
    local_grad = jnp.einsum('tacjhm,tabcjhk->abcjmhk', mixed_in, grad_r).reshape(NB, BLK, BLK)
    spread = jnp.einsum('tabcjhk,abcjmhk->tacjhm', grad_r, fac_r)
    dims_of = spread.shape
    spread = spread.reshape(dims_of[0], dims_of[1], dims_of[2], dims_of[3], dims_of[4], 2, BLK // 2)
    own_part = jnp.transpose(spread, (0, 1, 5, 2, 3, 4, 6))
    previous = (grad_r + own_part).astype(jnp.bfloat16).reshape(grad_next.shape)
    return previous, local_grad


def reference(hidden, weight, factors, cotangent):
    current = hidden
    inputs_kept = []
    for section_no in range(SECTIONS):
        inputs_kept.append(current)
        current = section_forward(current, factors[section_no], section_no)
    projected = jnp.dot(current, weight, preferred_element_type=jnp.float32).astype(jnp.bfloat16)
    grad_now = jnp.dot(cotangent, weight.T, preferred_element_type=jnp.float32).astype(jnp.bfloat16)
    factor_parts = [None] * SECTIONS
    for section_no in reversed(range(SECTIONS)):
        grad_now, local_grad = section_backward(inputs_kept[section_no], factors[section_no], grad_now, section_no)
        factor_parts[section_no] = local_grad
    factor_grad = jnp.stack(factor_parts) / jnp.float32(TOKENS)
    return projected, grad_now, factor_grad
```

```python
import jax
import jax.numpy as jnp
from jax import lax
from jax.experimental import pallas as pl
from jax.experimental.pallas import tpu as pltpu
from jax.sharding import PartitionSpec as P

MESH = pl.DeviceIdType.MESH
BF16 = jnp.bfloat16
F32 = jnp.float32

ROWS = 256
WIDTH = 448
HALF = 32
SECTIONS = 6
SIDE = 4
COL = 128
BLOCK = SIDE * COL
CHUNK = 128
QUART = 64
TILES = ((0, 128), (128, 128), (256, 128), (384, 64))

SCHEDULE = (
    "G FA FB S FA FB G FA G FB G FA FB G FA FB G FA FB G BA BB FA FB D5 R "
    "BA BB D4 D5 R BA BB D3 D4 D5 R BA BB D2 D3 D4 D5 R BA BB D1 D2 D3 D4 R "
    "BA BB D0 D1 D2 D3 R BA BB D0 D1 D2 D0 D1 D0"
)


def dot(a, b, contract):
    return lax.dot_general(a, b, (contract, ((), ())), preferred_element_type=F32)


def kernel(
    hid, w_hbm, fac, cot, proj, hgrad, fgrad,
    wv, cotg, par, xs, xp, gs, gp, fac_t, fac_p, ma, mb, mp, fg, fg_core, fg_half, fg_far,
    fg_all, acc, ra1, ra2, rb1, rb2, sa1, sa2, sb1, sb2, zr, w_sem, send, recv,
):
    dp = lax.axis_index("dp")
    t = lax.axis_index("tensor")
    y = lax.div(t, SIDE * SIDE)
    x = lax.rem(lax.div(t, SIDE), SIDE)
    z = lax.rem(t, SIDE)

    def ring(v, k):
        return lax.rem(v + k, SIDE)

    def at(yy, xx, zz):
        return (dp, (yy * SIDE + xx) * SIDE + zz)

    def y_dev(k):
        return at(ring(y, k), x, z)

    def x_dev(k):
        return at(y, ring(x, k), z)

    def z_dev(k):
        return at(y, x, ring(z, k))

    core_dev = (dp + 1 - 2 * lax.rem(dp, 2), t)
    far_dev = (lax.rem(dp + 2, 4), t)

    def bit_of(s):
        return lax.rem(lax.div(t, 1 << s), 2)

    def partner(s):
        return (dp, t + (1 << s) * (1 - 2 * bit_of(s)))

    def own_rows(s):
        return pl.ds(pl.multiple_of(HALF * bit_of(s), HALF), HALF)

    def other_rows(s):
        return pl.ds(pl.multiple_of(HALF - HALF * bit_of(s), HALF), HALF)

    started = []

    def copy(src, dst, dev):
        k = len(started)
        c = pltpu.make_async_remote_copy(
            src_ref=src, dst_ref=dst, send_sem=send.at[k], recv_sem=recv.at[k],
            device_id=dev, device_id_type=MESH,
        )
        c.start()
        started.append(c)
        return c

    w_copies = []
    for b in range(SIDE * SIDE):
        c = pltpu.make_async_copy(w_hbm.at[:, pl.ds(b * BLOCK, BLOCK)], wv.at[b], w_sem.at[b])
        c.start()
        w_copies.append(c)

    peers = [f(k) for f in (z_dev, x_dev, y_dev) for k in (1, 2, 3)] + [core_dev, far_dev]
    barrier = pltpu.get_barrier_semaphore()
    for dev in peers:
        pl.semaphore_signal(barrier, inc=1, device_id=dev, device_id_type=MESH)
    pl.semaphore_wait(barrier, len(peers))

    rows_a = (pl.ds(0, QUART), pl.ds(QUART, QUART))
    rows_b = (pl.ds(CHUNK, QUART), pl.ds(CHUNK + QUART, QUART))
    chunks = (pl.ds(0, CHUNK), pl.ds(CHUNK, CHUNK))

    def gather_phase(view, i, dev):
        r1 = copy(view(i, 0), view(i, 0), dev(1))
        l2 = copy(view(i, 1), view(i, 1), dev(3))
        r2 = copy(view(i, 1), view(i, 1), dev(1))
        l1 = copy(view(i, 0), view(i, 0), dev(3))
        yield
        left, right = ring(i, 3), ring(i, 1)
        r1.wait_recv()
        far1 = copy(view(left, 0), view(left, 0), dev(1))
        l2.wait_recv()
        far2 = copy(view(right, 1), view(right, 1), dev(3))
        yield
        r2.wait_recv()
        l1.wait_recv()
        yield
        far1.wait_recv()
        far2.wait_recv()
        yield

    def grad_dots(n, place):
        def step(k, carry):
            yy, xx = place(k)
            acc[...] += dot(cotg[yy, xx], wv[yy * SIDE + xx], ((1,), (1,)))
            return carry

        lax.fori_loop(0, n, step, 0)

    def near(k):
        return ring(y, 3 + lax.div(k, 3)), ring(x, 3 + lax.rem(k, 3))

    def gather():
        mine = pl.ds(pl.multiple_of(z * COL, COL), COL)
        z_copies = [copy(cot, cotg.at[y, x, :, mine], z_dev(k)) for k in (1, 2, 3)]
        cotg[y, x, :, mine] = cot[...]
        acc[...] = jnp.zeros_like(acc)
        yield
        for c in z_copies:
            c.wait_recv()
        pa = gather_phase(lambda i, h: cotg.at[y, i, rows_a[h], :], x, x_dev)
        pb = gather_phase(lambda i, h: cotg.at[i, x, rows_b[h], :], y, y_dev)
        next(pa), next(pb)
        yield
        next(pa), next(pb)
        yield
        next(pa), next(pb)
        next(pa), next(pb)
        pa = gather_phase(lambda i, h: cotg.at[i, :, rows_a[h], :], y, y_dev)
        pb = gather_phase(lambda i, h: cotg.at[:, i, rows_b[h], :], x, x_dev)
        next(pa), next(pb)
        yield
        next(pa), next(pb)
        yield
        next(pa), next(pb)
        for c in w_copies:
            c.wait()
        grad_dots(9, near)
        yield
        next(pa), next(pb)
        grad_dots(
            7,
            lambda k: (
                ring(y, jnp.where(k < 4, 2, k - 1)),
                ring(x, jnp.where(k < 4, k, 2)),
            ),
        )
        gs[SECTIONS - 1] = acc[...].astype(BF16)
        yield

    diag = (
        lax.broadcasted_iota(jnp.int32, (COL, WIDTH), 0) // HALF
        == lax.rem(lax.broadcasted_iota(jnp.int32, (COL, WIDTH), 1), COL) // HALF
    )

    def spread(part):
        return jnp.where(diag, jnp.concatenate([part] * 4, axis=0), jnp.zeros((), BF16))

    fac_copies = [None] * SECTIONS

    def setup():
        for s in range(SECTIONS):
            fac_t[s] = jnp.concatenate([fac[s, j] for j in range(7)], axis=1)
        for s in reversed(range(SECTIONS)):
            fac_copies[s] = copy(fac_t.at[s, other_rows(s), :], fac_p.at[s], partner(s))
        for s in range(SECTIONS):
            ma[s] = spread(fac_t[s, own_rows(s), :])
            mb[s] = spread(fac_t[s, other_rows(s), :])
        yield

    def x_ref(s):
        return hid if s == 0 else xs.at[s - 1]

    def forward(rows):
        for s in range(SECTIONS):
            c = copy(x_ref(s).at[rows, :], xp.at[s, rows, :], partner(s))
            yield
            c.wait_recv()
            src, dst = x_ref(s), x_ref(s + 1)
            for lo, w in TILES:
                own = src[rows, lo : lo + w]
                mix = dot(own, ma[s, 0:w, lo : lo + w], ((1,), (0,)))
                mix += dot(xp[s, rows, lo : lo + w], mb[s, 0:w, lo : lo + w], ((1,), (0,)))
                dst[rows, lo : lo + w] = (own.astype(F32) + mix).astype(BF16)
        yield

    def proj_dots(n, place):
        def step(k, carry):
            yy, xx = place(k)
            out = dot(x_ref(SECTIONS)[...], wv[yy * SIDE + xx], ((1,), (0,)))
            par[yy, xx] = out.astype(BF16)
            return carry

        lax.fori_loop(0, n, step, 0)

    def add_to(ref, *others):
        total = ref[...].astype(F32)
        for o in others:
            total += o[...].astype(F32)
        ref[...] = total.astype(BF16)

    def scatter_phase(view, i, buf1, buf2, dev):
        p1, p2, m1 = ring(i, 1), ring(i, 2), ring(i, 3)
        a = copy(view(p2, 0), buf1.at[0], dev(1))
        b = copy(view(p2, 1), buf1.at[1], dev(3))
        yield
        c = copy(view(p1, 1), buf2.at[0, 1], dev(1))
        d = copy(view(m1, 0), buf2.at[1, 0], dev(3))
        yield
        a.wait_recv()
        add_to(view(p1, 0), buf1.at[0])
        e = copy(view(p1, 0), buf2.at[0, 0], dev(1))
        b.wait_recv()
        add_to(view(m1, 1), buf1.at[1])
        f = copy(view(m1, 1), buf2.at[1, 1], dev(3))
        yield
        c.wait_recv()
        f.wait_recv()
        add_to(view(i, 1), buf2.at[0, 1], buf2.at[1, 1])
        d.wait_recv()
        e.wait_recv()
        add_to(view(i, 0), buf2.at[0, 0], buf2.at[1, 0])
        yield

    def scatter():
        pa = scatter_phase(lambda i, h: par.at[i, :, rows_a[h], :], y, ra1, ra2, y_dev)
        pb = scatter_phase(lambda i, h: par.at[:, i, rows_b[h], :], x, rb1, rb2, x_dev)
        proj_dots(4, lambda k: (ring(y, 2), ring(x, k)))
        next(pa)
        proj_dots(3, lambda k: (ring(y, 3 + k), ring(x, 2)))
        next(pb)
        proj_dots(6, lambda k: (ring(y, 1 + 2 * lax.div(k, 3)), ring(x, 3 + lax.rem(k, 3))))
        next(pa)
        proj_dots(3, lambda k: (y, ring(x, 3 + k)))
        next(pb)
        yield
        next(pa), next(pb)
        yield
        next(pa), next(pb)
        pa = scatter_phase(lambda i, h: par.at[y, i, rows_a[h], :], x, sa1, sa2, x_dev)
        pb = scatter_phase(lambda i, h: par.at[i, x, rows_b[h], :], y, sb1, sb2, y_dev)
        next(pa), next(pb)
        next(pa), next(pb)
        yield
        next(pa), next(pb)
        yield
        next(pa), next(pb)

        def columns(zz):
            return pl.ds(pl.multiple_of(zz * COL, COL), COL)

        last = [
            [
                copy(par.at[y, x, chunks[h], columns(ring(z, k))], zr.at[h, k - 1], z_dev(k))
                for k in (1, 2, 3)
            ]
            for h in (0, 1)
        ]
        yield
        for h in (0, 1):
            total = par[y, x, chunks[h], columns(z)].astype(F32)
            for k in (1, 2, 3):
                last[h][k - 1].wait_recv()
                total += zr[h, k - 1].astype(F32)
            proj[chunks[h], :] = total.astype(BF16)
        yield

    def backward(rows, first):
        for s in reversed(range(SECTIONS)):
            c = copy(gs.at[s, rows, :], gp.at[s, rows, :], partner(s))
            if first:
                fac_copies[s].wait_recv()
                mp[s] = spread(fac_p[s])
            yield
            c.wait_recv()
            for lo, w in TILES:
                own = gs[s, rows, lo : lo + w]
                back = dot(own, ma[s, 0:w, lo : lo + w], ((1,), (1,)))
                back += dot(gp[s, rows, lo : lo + w], mp[s, 0:w, lo : lo + w], ((1,), (1,)))
                new = (own.astype(F32) + back).astype(BF16)
                if s == 0:
                    hgrad[rows, lo : lo + w] = new
                else:
                    gs[s - 1, rows, lo : lo + w] = new
        yield

    core = lax.rem(dp, 2)
    keep = pl.ds(pl.multiple_of(HALF * core, HALF), HALF)
    give = pl.ds(pl.multiple_of(HALF - HALF * core, HALF), HALF)

    def factor(s):
        for act, rows in ((x_ref(s), own_rows(s)), (xp.at[s], other_rows(s))):
            for lo, w in TILES:
                full = dot(act[:, lo : lo + w], gs[s, :, lo : lo + w], ((0,), (0,)))
                full = jnp.where(diag[:w, :w], full, 0.0)
                total = full[0:HALF]
                for g in range(1, w // HALF):
                    total += full[g * HALF : (g + 1) * HALF]
                fg[s, rows, lo : lo + w] = total
        a = copy(fg.at[s, give, :], fg_core.at[s], core_dev)
        yield
        a.wait_recv()
        fg_half[s] = (fg[s, keep, :] + fg_core[s]).astype(BF16)
        b = copy(fg_half.at[s], fg_far.at[s], far_dev)
        yield
        b.wait_recv()
        fg_all[s, keep, :] = fg_half[s].astype(F32) + fg_far[s].astype(F32)
        c = copy(fg_all.at[s, keep, :], fg_all.at[s, keep, :], core_dev)
        yield
        c.wait_recv()
        fgrad[s] = fg_all[s]
        yield

    chains = {
        "G": gather(),
        "S": setup(),
        "FA": forward(chunks[0]),
        "FB": forward(chunks[1]),
        "BA": backward(chunks[0], True),
        "BB": backward(chunks[1], False),
        "R": scatter(),
    }
    for s in range(SECTIONS):
        chains[f"D{s}"] = factor(s)
    for name in SCHEDULE.split():
        next(chains[name], None)
    for chain in chains.values():
        for _ in chain:
            pass
    assert len(started) == COPIES
    for c in started:
        c.wait_send()


COPIES = 105


def body(hidden, weight, factors, cotangent):
    vmem = pl.BlockSpec(memory_space=pltpu.VMEM)
    part = (SIDE, QUART, BLOCK)
    scratch = [
        ((SIDE * SIDE, WIDTH, BLOCK), BF16),
        ((SIDE, SIDE, ROWS, BLOCK), BF16),
        ((SIDE, SIDE, ROWS, BLOCK), BF16),
        ((SECTIONS, ROWS, WIDTH), BF16),
        ((SECTIONS, ROWS, WIDTH), BF16),
        ((SECTIONS, ROWS, WIDTH), BF16),
        ((SECTIONS, ROWS, WIDTH), BF16),
        ((SECTIONS, 2 * HALF, WIDTH), BF16),
        ((SECTIONS, HALF, WIDTH), BF16),
        ((SECTIONS, COL, WIDTH), BF16),
        ((SECTIONS, COL, WIDTH), BF16),
        ((SECTIONS, COL, WIDTH), BF16),
        ((SECTIONS, 2 * HALF, WIDTH), F32),
        ((SECTIONS, HALF, WIDTH), F32),
        ((SECTIONS, HALF, WIDTH), BF16),
        ((SECTIONS, HALF, WIDTH), BF16),
        ((SECTIONS, 2 * HALF, WIDTH), F32),
        ((ROWS, WIDTH), F32),
        ((2,) + part, BF16),
        ((2, 2) + part, BF16),
        ((2,) + part, BF16),
        ((2, 2) + part, BF16),
        ((2, QUART, BLOCK), BF16),
        ((2, 2, QUART, BLOCK), BF16),
        ((2, QUART, BLOCK), BF16),
        ((2, 2, QUART, BLOCK), BF16),
        ((2, 3, CHUNK, COL), BF16),
    ]
    proj, hgrad, fgrad = pl.pallas_call(
        kernel,
        out_shape=(
            jax.ShapeDtypeStruct((ROWS, COL), BF16),
            jax.ShapeDtypeStruct((ROWS, WIDTH), BF16),
            jax.ShapeDtypeStruct((SECTIONS, 2 * HALF, WIDTH), F32),
        ),
        in_specs=[vmem, pl.BlockSpec(memory_space=pl.ANY), vmem, vmem],
        out_specs=(vmem, vmem, vmem),
        scratch_shapes=[pltpu.VMEM(*one) for one in scratch]
        + [
            pltpu.SemaphoreType.DMA((SIDE * SIDE,)),
            pltpu.SemaphoreType.DMA((COPIES,)),
            pltpu.SemaphoreType.DMA((COPIES,)),
        ],
        compiler_params=pltpu.CompilerParams(
            collective_id=0, has_side_effects=True, vmem_limit_bytes=56 * 1024 * 1024
        ),
        name="butterfly",
    )(hidden, weight, factors, cotangent)
    grad = fgrad.reshape(SECTIONS, 2 * HALF, 7, 2 * HALF).transpose(0, 2, 1, 3)
    tokens = ROWS * lax.axis_size("dp")
    return proj, hgrad, grad / jnp.float32(tokens)


def solution(mesh):
    return jax.shard_map(
        body,
        mesh=mesh,
        in_specs=(
            P("dp", "tensor"),
            P("tensor", None),
            P(None, "tensor", None, None),
            P("dp", "tensor"),
        ),
        out_specs=(P("dp", "tensor"), P("dp", "tensor"), P(None, "tensor", None, None)),
        check_vma=False,
    )
```

```python
import jax
import jax.numpy as jnp
from jax import lax
from jax.experimental import pallas as pl
from jax.experimental.pallas import tpu as pltpu
from jax.sharding import PartitionSpec as P

MESH = pl.DeviceIdType.MESH
BF16 = jnp.bfloat16
F32 = jnp.float32

ROWS = 256
WIDTH = 448
LANES = 7
HALF = 32
SECTIONS = 6
SIDE = 4
COL = 128
BLOCK = SIDE * COL
CHUNK = 128
QUART = 64
TILES = ((0, 128), (128, 128), (256, 128), (384, 64))
PARTS = ((0, 1), (2, 3))

SCHEDULE = (
    ("G", "F0", "F1", "S", "F0", "F1", "G", "F0", "F1", "G", "F0", "F1", "G", "F0", "F1"),
    ("F0", "F1", "G", "G", "B0", "B1", "F0", "F1", "R"),
    ("D5", "B0", "B1", "D4", "D5", "R", "B0", "B1", "D3", "D4", "D5", "R"),
    ("B0", "B1", "D2", "D3", "D4", "R", "B0", "B1", "D1", "D2", "D3", "R"),
    ("B0", "B1", "D0", "D1", "D2", "D0", "D1", "B0", "B1", "D0"),
)


def dot(a, b, contract=((1,), (0,))):
    return lax.dot_general(a, b, (contract, ((), ())), preferred_element_type=F32)


NT = ((1,), (1,))


def kernel(
    hid, w_hbm, fac_hbm, cot_hbm, proj_out, hgrad_out, fgrad_out,
    wv, cotv, facv, cotg, par, xs, xp, gs, gp, fac_t, fac_p, ma, mat, mbt, mp,
    fg, fg_core, fg_half, fg_far, fg_all, acc, ra1, ra2, rb1, rb2, sa, sb, zr,
    proj, hgrad, fgrad, in_sem, out_sem, send, recv,
):
    dp = lax.axis_index("dp")
    t = lax.axis_index("tensor")
    y = lax.div(t, SIDE * SIDE)
    x = lax.rem(lax.div(t, SIDE), SIDE)
    z = lax.rem(t, SIDE)
    core = lax.rem(dp, 2)

    def ring(v, k):
        return lax.rem(v + k, SIDE)

    def at(yy, xx, zz):
        return (dp, (yy * SIDE + xx) * SIDE + zz)

    def y_dev(k):
        return at(ring(y, k), x, z)

    def x_dev(k):
        return at(y, ring(x, k), z)

    def z_dev(k):
        return at(y, x, ring(z, k))

    far = lax.rem(dp + 2, 4)
    core_dev = (dp + 1 - 2 * core, t)
    far_dev = (far, t)
    cross_dev = (far + 1 - 2 * core, t)

    def bit_of(s):
        return lax.rem(lax.div(t, 1 << s), 2)

    def partner(s):
        return (dp, t + (1 << s) * (1 - 2 * bit_of(s)))

    def own_rows(s):
        return pl.ds(pl.multiple_of(HALF * bit_of(s), HALF), HALF)

    def other_rows(s):
        return pl.ds(pl.multiple_of(HALF - HALF * bit_of(s), HALF), HALF)

    started = []

    def copy(src, dst, dev):
        k = len(started)
        c = pltpu.make_async_remote_copy(
            src_ref=src, dst_ref=dst, send_sem=send.at[k], recv_sem=recv.at[k],
            device_id=dev, device_id_type=MESH,
        )
        c.start()
        started.append(c)
        return c

    def fetch(src, dst, k):
        c = pltpu.make_async_copy(src, dst, in_sem.at[k])
        c.start()
        return c

    cot_copy = fetch(cot_hbm, cotv, 0)
    hid_copy = fetch(hid, xs.at[0], 1)
    fac_copy = fetch(fac_hbm, facv, 2)
    w_copies = [
        fetch(w_hbm.at[:, pl.ds(b * BLOCK, BLOCK)], wv.at[b], 3 + b) for b in range(SIDE * SIDE)
    ]
    stored = []

    def put(src, dst):
        c = pltpu.make_async_copy(src, dst, out_sem.at[len(stored)])
        c.start()
        stored.append(c)

    peers = [f(k) for f in (z_dev, x_dev, y_dev) for k in (1, 2, 3)]
    peers += [core_dev, far_dev, cross_dev]
    barrier = pltpu.get_barrier_semaphore()
    for dev in peers:
        pl.semaphore_signal(barrier, inc=1, device_id=dev, device_id_type=MESH)
    pl.semaphore_wait(barrier, len(peers))

    half_a, half_b = pl.ds(0, CHUNK), pl.ds(CHUNK, CHUNK)
    rows_a = (pl.ds(0, QUART), pl.ds(QUART, QUART))
    rows_b = (pl.ds(CHUNK, QUART), pl.ds(CHUNK + QUART, QUART))

    def gather_phase(view, i, dev):
        r1 = copy(view(i, 0), view(i, 0), dev(1))
        l2 = copy(view(i, 1), view(i, 1), dev(3))
        r2 = copy(view(i, 1), view(i, 1), dev(1))
        l1 = copy(view(i, 0), view(i, 0), dev(3))
        yield
        left, right = ring(i, 3), ring(i, 1)
        r1.wait_recv()
        far1 = copy(view(left, 0), view(left, 0), dev(1))
        l2.wait_recv()
        far2 = copy(view(right, 1), view(right, 1), dev(3))
        yield
        r2.wait_recv()
        l1.wait_recv()
        yield
        far1.wait_recv()
        far2.wait_recv()
        yield

    def grad_dots(n, place):
        def step(k, carry):
            yy, xx = place(k)
            acc[...] += dot(wv[yy * SIDE + xx], cotg[yy, xx], NT)
            return carry

        lax.fori_loop(0, n, step, 0)

    def columns(zz):
        return pl.ds(pl.multiple_of(zz * COL, COL), COL)

    def gather():
        cot_copy.wait()
        copies = [copy(cotv, cotg.at[y, x, :, columns(z)], z_dev(k)) for k in (1, 2, 3)]
        cotg[y, x, :, columns(z)] = cotv[...]
        acc[...] = jnp.zeros_like(acc)
        yield
        for c in copies:
            c.wait_recv()
        here_a, here_b = cotg.at[y, x, half_a, :], cotg.at[y, x, half_b, :]
        copies = []
        for k in (1, 3, 2):
            copies.append(copy(here_a, here_a, x_dev(k)))
            copies.append(copy(here_b, here_b, y_dev(k)))
        yield
        for c in copies:
            c.wait_recv()
        pa = gather_phase(lambda i, h: cotg.at[i, :, rows_a[h], :], y, y_dev)
        pb = gather_phase(lambda i, h: cotg.at[:, i, rows_b[h], :], x, x_dev)
        next(pa), next(pb)
        yield
        next(pa), next(pb)
        yield
        next(pa), next(pb)
        for c in w_copies:
            c.wait()
        grad_dots(9, lambda k: (ring(y, 3 + lax.div(k, 3)), ring(x, 3 + lax.rem(k, 3))))
        yield
        next(pa), next(pb)
        grad_dots(
            7,
            lambda k: (
                ring(y, jnp.where(k < 4, 2, k - 1)),
                ring(x, jnp.where(k < 4, k, 2)),
            ),
        )
        gs[SECTIONS - 1] = acc[...].astype(BF16)
        yield

    diag = (
        lax.broadcasted_iota(jnp.int32, (COL, WIDTH), 0) // HALF
        == lax.rem(lax.broadcasted_iota(jnp.int32, (COL, WIDTH), 1), COL) // HALF
    )

    def spread(part):
        return jnp.where(diag, jnp.concatenate([part] * 4, axis=0), jnp.zeros((), BF16))

    def turned(ref, full):
        for lo, w in TILES:
            ref[lo : lo + w, 0:w] = full[0:w, lo : lo + w].T

    fac_copies = [None] * SECTIONS

    def setup():
        fac_copy.wait()
        for s in range(SECTIONS):
            fac_t[s] = jnp.concatenate([facv[s, j] for j in range(LANES)], axis=1)
        for s in reversed(range(SECTIONS)):
            fac_copies[s] = copy(fac_t.at[s, other_rows(s), :], fac_p.at[s], partner(s))
        for s in range(SECTIONS):
            own = spread(fac_t[s, own_rows(s), :])
            ma[s] = own
            turned(mat.at[s], own)
            turned(mbt.at[s], spread(fac_t[s, other_rows(s), :]))
        yield

    def span(part):
        lo = TILES[part[0]][0]
        return pl.ds(lo, TILES[part[-1]][0] + TILES[part[-1]][1] - lo)

    def forward(part):
        if part is PARTS[0]:
            hid_copy.wait()
        for s in range(SECTIONS):
            rows = span(part)
            c = copy(xs.at[s, rows, :], xp.at[s, rows, :], partner(s))
            yield
            c.wait_recv()
            for i in part:
                lo, w = TILES[i]
                own = xs[s, lo : lo + w, :]
                mix = dot(mat[s, lo : lo + w, 0:w], own)
                mix += dot(mbt[s, lo : lo + w, 0:w], xp[s, lo : lo + w, :])
                xs[s + 1, lo : lo + w, :] = (own.astype(F32) + mix).astype(BF16)
        yield

    def proj_dots(n, place):
        def step(k, carry):
            yy, xx = place(k)
            par[yy, xx] = dot(proj_in[0], wv[yy * SIDE + xx]).astype(BF16)
            return carry

        lax.fori_loop(0, n, step, 0)

    proj_in = [None]

    def add_to(ref, *others):
        total = ref[...].astype(F32)
        for o in others:
            total += o[...].astype(F32)
        ref[...] = total.astype(BF16)

    def scatter_phase(view, i, buf1, buf2, dev):
        p1, p2, m1 = ring(i, 1), ring(i, 2), ring(i, 3)
        a = copy(view(p2, 0), buf1.at[0], dev(1))
        b = copy(view(p2, 1), buf1.at[1], dev(3))
        yield
        c = copy(view(p1, 1), buf2.at[0, 1], dev(1))
        d = copy(view(m1, 0), buf2.at[1, 0], dev(3))
        yield
        a.wait_recv()
        add_to(view(p1, 0), buf1.at[0])
        e = copy(view(p1, 0), buf2.at[0, 0], dev(1))
        b.wait_recv()
        add_to(view(m1, 1), buf1.at[1])
        f = copy(view(m1, 1), buf2.at[1, 1], dev(3))
        yield
        c.wait_recv()
        f.wait_recv()
        add_to(view(i, 1), buf2.at[0, 1], buf2.at[1, 1])
        d.wait_recv()
        e.wait_recv()
        add_to(view(i, 0), buf2.at[0, 0], buf2.at[1, 0])
        yield

    def scatter():
        pa = scatter_phase(lambda i, h: par.at[i, :, rows_a[h], :], y, ra1, ra2, y_dev)
        pb = scatter_phase(lambda i, h: par.at[:, i, rows_b[h], :], x, rb1, rb2, x_dev)
        proj_in[0] = xs[SECTIONS].T
        proj_dots(4, lambda k: (ring(y, 2), ring(x, k)))
        next(pa)
        proj_dots(3, lambda k: (ring(y, 3 + k), ring(x, 2)))
        next(pb)
        proj_dots(6, lambda k: (ring(y, 1 + 2 * lax.div(k, 3)), ring(x, 3 + lax.rem(k, 3))))
        next(pa)
        proj_dots(3, lambda k: (y, ring(x, 3 + k)))
        next(pb)
        yield
        next(pa), next(pb)
        yield
        next(pa), next(pb)
        copies = []
        for k in (2, 1, 3):
            copies.append(copy(par.at[y, ring(x, k), half_a, :], sa.at[k - 1], x_dev(k)))
            copies.append(copy(par.at[ring(y, k), x, half_b, :], sb.at[k - 1], y_dev(k)))
        yield
        for c in copies:
            c.wait_recv()
        add_to(par.at[y, x, half_a, :], sa.at[0], sa.at[1], sa.at[2])
        add_to(par.at[y, x, half_b, :], sb.at[0], sb.at[1], sb.at[2])
        copies = [
            copy(par.at[y, x, :, columns(ring(z, k))], zr.at[k - 1], z_dev(k)) for k in (1, 2, 3)
        ]
        yield
        total = par[y, x, :, columns(z)].astype(F32)
        for k in (1, 2, 3):
            copies[k - 1].wait_recv()
            total += zr[k - 1].astype(F32)
        proj[...] = total.astype(BF16)
        put(proj, proj_out)
        yield

    def backward(part):
        for s in reversed(range(SECTIONS)):
            rows = span(part)
            c = copy(gs.at[s, rows, :], gp.at[s, rows, :], partner(s))
            if part is PARTS[0]:
                fac_copies[s].wait_recv()
                mp[s] = spread(fac_p[s])
            yield
            c.wait_recv()
            for i in part:
                lo, w = TILES[i]
                own = gs[s, lo : lo + w, :]
                back = dot(ma[s, 0:w, lo : lo + w], own)
                back += dot(mp[s, 0:w, lo : lo + w], gp[s, lo : lo + w, :])
                new = (own.astype(F32) + back).astype(BF16)
                if s == 0:
                    hgrad[lo : lo + w, :] = new
                else:
                    gs[s - 1, lo : lo + w, :] = new
        put(hgrad.at[rows, :], hgrad_out.at[rows, :])
        yield

    keep = pl.ds(pl.multiple_of(HALF * core, HALF), HALF)
    give = pl.ds(pl.multiple_of(HALF - HALF * core, HALF), HALF)

    def factor(s):
        for act, rows in ((xs.at[s], own_rows(s)), (xp.at[s], other_rows(s))):
            for lo, w in TILES:
                full = dot(act[lo : lo + w, :], gs[s, lo : lo + w, :], NT)
                full = jnp.where(diag[:w, :w], full, 0.0)
                total = full[0:HALF]
                for g in range(1, w // HALF):
                    total += full[g * HALF : (g + 1) * HALF]
                fg[s, rows, lo : lo + w] = total
        if s == 0:
            a = copy(fg.at[s], fg_all.at[s], core_dev)
            yield
            a.wait_recv()
            chip = (fg[s] + fg_all[s]).astype(BF16)
            fg_half[...] = chip
            b = copy(fg_half.at[keep, :], fg_far.at[s, keep, :], far_dev)
            c = copy(fg_half.at[keep, :], fg_far.at[s, keep, :], cross_dev)
            yield
            b.wait_recv()
            c.wait_recv()
            total = chip.astype(F32) + fg_far[s].astype(F32)
        else:
            a = copy(fg.at[s, give, :], fg_core.at[s], core_dev)
            yield
            a.wait_recv()
            chip = (fg[s, keep, :] + fg_core[s]).astype(BF16)
            fg_far[s, give, :] = chip
            b = copy(fg_far.at[s, give, :], fg_far.at[s, keep, :], far_dev)
            yield
            b.wait_recv()
            fg_all[s, keep, :] = chip.astype(F32) + fg_far[s, keep, :].astype(F32)
            c = copy(fg_all.at[s, keep, :], fg_all.at[s, keep, :], core_dev)
            yield
            c.wait_recv()
            total = fg_all[s]
        total = total * (1.0 / (4 * ROWS))
        for j in range(LANES):
            fgrad[s, j] = total[:, 2 * HALF * j : 2 * HALF * (j + 1)]
        put(fgrad.at[s], fgrad_out.at[s])
        yield

    chains = {"G": gather(), "S": setup(), "R": scatter()}
    for n, part in enumerate(PARTS):
        chains[f"F{n}"] = forward(part)
        chains[f"B{n}"] = backward(part)
    for s in range(SECTIONS):
        chains[f"D{s}"] = factor(s)
    for name in sum(SCHEDULE, ()):
        next(chains[name], None)
    for chain in chains.values():
        for _ in chain:
            pass
    assert len(started) == COPIES
    for c in started:
        c.wait_send()
    for c in stored:
        c.wait()


COPIES = 3 + 6 + 12 + 6 + 12 * len(PARTS) + 12 + 6 + 3 + 18
STORES = 1 + len(PARTS) + SECTIONS


def body(hidden, weight, factors, cotangent):
    anywhere = pl.BlockSpec(memory_space=pl.ANY)
    part = (SIDE, QUART, BLOCK)
    acts = (SECTIONS, WIDTH, ROWS)
    scratch = [
        ((SIDE * SIDE, WIDTH, BLOCK), BF16),
        ((ROWS, COL), BF16),
        ((SECTIONS, LANES, 2 * HALF, 2 * HALF), BF16),
        ((SIDE, SIDE, ROWS, BLOCK), BF16),
        ((SIDE, SIDE, ROWS, BLOCK), BF16),
        ((SECTIONS + 1, WIDTH, ROWS), BF16),
        (acts, BF16),
        (acts, BF16),
        (acts, BF16),
        ((SECTIONS, 2 * HALF, WIDTH), BF16),
        ((SECTIONS, HALF, WIDTH), BF16),
        ((SECTIONS, COL, WIDTH), BF16),
        ((SECTIONS, WIDTH, COL), BF16),
        ((SECTIONS, WIDTH, COL), BF16),
        ((SECTIONS, COL, WIDTH), BF16),
        ((SECTIONS, 2 * HALF, WIDTH), F32),
        ((SECTIONS, HALF, WIDTH), F32),
        ((2 * HALF, WIDTH), BF16),
        ((SECTIONS, 2 * HALF, WIDTH), BF16),
        ((SECTIONS, 2 * HALF, WIDTH), F32),
        ((WIDTH, ROWS), F32),
        ((2,) + part, BF16),
        ((2, 2) + part, BF16),
        ((2,) + part, BF16),
        ((2, 2) + part, BF16),
        ((3, CHUNK, BLOCK), BF16),
        ((3, CHUNK, BLOCK), BF16),
        ((3, ROWS, COL), BF16),
        ((ROWS, COL), BF16),
        ((WIDTH, ROWS), BF16),
        ((SECTIONS, LANES, 2 * HALF, 2 * HALF), F32),
    ]
    proj, hgrad, fgrad = pl.pallas_call(
        kernel,
        out_shape=(
            jax.ShapeDtypeStruct((ROWS, COL), BF16),
            jax.ShapeDtypeStruct((WIDTH, ROWS), BF16),
            jax.ShapeDtypeStruct((SECTIONS, LANES, 2 * HALF, 2 * HALF), F32),
        ),
        in_specs=[anywhere] * 4,
        out_specs=(anywhere,) * 3,
        scratch_shapes=[pltpu.VMEM(*one) for one in scratch]
        + [
            pltpu.SemaphoreType.DMA((3 + SIDE * SIDE,)),
            pltpu.SemaphoreType.DMA((STORES,)),
            pltpu.SemaphoreType.DMA((COPIES,)),
            pltpu.SemaphoreType.DMA((COPIES,)),
        ],
        compiler_params=pltpu.CompilerParams(
            collective_id=0, has_side_effects=True, vmem_limit_bytes=56 * 1024 * 1024
        ),
        name="butterfly",
    )(hidden.T, weight, factors, cotangent)
    return proj, hgrad.T, fgrad


def solution(mesh):
    return jax.shard_map(
        body,
        mesh=mesh,
        in_specs=(
            P("dp", "tensor"),
            P("tensor", None),
            P(None, "tensor", None, None),
            P("dp", "tensor"),
        ),
        out_specs=(P("dp", "tensor"), P("dp", "tensor"), P(None, "tensor", None, None)),
        check_vma=False,
    )
```

```python
import jax
import jax.numpy as jnp
from jax import lax
from jax.experimental import pallas as pl
from jax.experimental.pallas import tpu as pltpu
from jax.sharding import PartitionSpec as P

MESH = pl.DeviceIdType.MESH
BF16 = jnp.bfloat16
F32 = jnp.float32

ROWS = 256
WIDTH = 448
LANES = 7
HALF = 32
SECTIONS = 6
SIDE = 4
COL = 128
BLOCK = SIDE * COL
CHUNK = 128
TILES = ((0, 128), (128, 128), (256, 128), (384, 64))
PARTS = ((0,), (1,), (2, 3))

GROUPS = 2

SCHEDULE = (
    ("G", "F2", "S", "F1", "F0", "G", "GB0", "GA0", "GB1", "GA1"),
    ("F0", "GA0", "GB1", "F2", "F1", "GB0", "GA1", "GA1", "F0", "GB0"),
    ("GB1", "GA0", "GD", "GA0", "GB1", "GB0", "GA1", "GD", "B0", "F2"),
    ("B1", "F0", "B2", "F2", "B0", "F1", "F0", "B1", "B2", "B0"),
    ("F2", "F1", "B0", "F0", "B2", "F1", "B1", "B0", "D3", "F2"),
    ("B2", "F1", "F2", "B1", "D3", "F0", "D4", "F1", "R", "R"),
    ("B1", "B2", "D5", "R", "R", "RA0", "B0", "D2", "B1", "D3"),
    ("D5", "RB1", "RB0", "D1", "B0", "B2", "D0", "D1", "RA1", "D5"),
    ("D3", "D2", "D0", "RB1", "D4", "RA0", "D2", "D5", "RB0", "RA1"),
    ("D1", "RB1", "RA0", "RB0", "RA1", "D0", "D4", "D2", "RB1", "RB0"),
    ("RA0", "B1", "B2", "D1", "D4", "RA1"),
)


def dot(a, b, contract=((1,), (0,))):
    return lax.dot_general(a, b, (contract, ((), ())), preferred_element_type=F32)


NT = ((1,), (1,))


def kernel(
    hid, w_hbm, fac_hbm, cot_hbm, proj_out, hgrad_out, fgrad_out,
    wv, cotv, facv, cotg, par, xs, xp, gs, gp, fac_t, fac_p, ma, mat, mbt, mp,
    fg, fg_core, fg_half, fg_far, fg_all, acc, buf1, buf2, buf3, zr,
    proj, hgrad, fgrad, in_sem, out_sem, send, recv,
):
    dp = lax.axis_index("dp")
    t = lax.axis_index("tensor")
    y = lax.div(t, SIDE * SIDE)
    x = lax.rem(lax.div(t, SIDE), SIDE)
    z = lax.rem(t, SIDE)
    core = lax.rem(dp, 2)

    def ring(v, k):
        return lax.rem(v + k, SIDE)

    def at(yy, xx, zz):
        return (dp, (yy * SIDE + xx) * SIDE + zz)

    def y_dev(k):
        return at(ring(y, k), x, z)

    def x_dev(k):
        return at(y, ring(x, k), z)

    def z_dev(k):
        return at(y, x, ring(z, k))

    far = lax.rem(dp + 2, 4)
    core_dev = (dp + 1 - 2 * core, t)
    far_dev = (far, t)
    cross_dev = (far + 1 - 2 * core, t)

    def bit_of(s):
        return lax.rem(lax.div(t, 1 << s), 2)

    def partner(s):
        return (dp, t + (1 << s) * (1 - 2 * bit_of(s)))

    def own_rows(s):
        return pl.ds(pl.multiple_of(HALF * bit_of(s), HALF), HALF)

    def other_rows(s):
        return pl.ds(pl.multiple_of(HALF - HALF * bit_of(s), HALF), HALF)

    started = []

    def copy(src, dst, dev):
        k = len(started)
        c = pltpu.make_async_remote_copy(
            src_ref=src, dst_ref=dst, send_sem=send.at[k], recv_sem=recv.at[k],
            device_id=dev, device_id_type=MESH,
        )
        c.start()
        started.append(c)
        return c

    def fetch(src, dst, k):
        c = pltpu.make_async_copy(src, dst, in_sem.at[k])
        c.start()
        return c

    cot_copy = fetch(cot_hbm, cotv, 0)
    hid_copy = fetch(hid, xs.at[0], 1)
    fac_copy = fetch(fac_hbm, facv, 2)
    w_copies = [
        fetch(w_hbm.at[:, pl.ds(b * BLOCK, BLOCK)], wv.at[b], 3 + b) for b in range(SIDE * SIDE)
    ]
    stored = []

    def put(src, dst):
        c = pltpu.make_async_copy(src, dst, out_sem.at[len(stored)])
        c.start()
        stored.append(c)

    peers = [f(k) for f in (z_dev, x_dev, y_dev) for k in (1, 2, 3)]
    peers += [core_dev, far_dev, cross_dev]
    barrier = pltpu.get_barrier_semaphore()
    for dev in peers:
        pl.semaphore_signal(barrier, inc=1, device_id=dev, device_id_type=MESH)
    pl.semaphore_wait(barrier, len(peers))

    size = CHUNK // GROUPS
    piece = size // 2

    def group(h, g):
        return pl.ds(CHUNK * h + size * g, size)

    def piece_of(h, g, p):
        return pl.ds(CHUNK * h + size * g + piece * p, piece)

    def gather_phase(view, i, dev):
        r1 = copy(view(i, 0), view(i, 0), dev(1))
        l2 = copy(view(i, 1), view(i, 1), dev(3))
        r2 = copy(view(i, 1), view(i, 1), dev(1))
        l1 = copy(view(i, 0), view(i, 0), dev(3))
        yield
        left, right = ring(i, 3), ring(i, 1)
        r1.wait_recv()
        far1 = copy(view(left, 0), view(left, 0), dev(1))
        l2.wait_recv()
        far2 = copy(view(right, 1), view(right, 1), dev(3))
        yield
        r2.wait_recv()
        l1.wait_recv()
        yield
        far1.wait_recv()
        far2.wait_recv()
        yield

    def grad_dots(n, place):
        def step(k, carry):
            yy, xx = place(k)
            acc[...] += dot(wv[yy * SIDE + xx], cotg[yy, xx], NT)
            return carry

        lax.fori_loop(0, n, step, 0)

    def columns(zz):
        return pl.ds(pl.multiple_of(zz * COL, COL), COL)

    second = {}

    def gather():
        cot_copy.wait()
        copies = [copy(cotv, cotg.at[y, x, :, columns(z)], z_dev(k)) for k in (1, 2, 3)]
        cotg[y, x, :, columns(z)] = cotv[...]
        acc[...] = jnp.zeros_like(acc)
        yield
        for c in copies:
            c.wait_recv()
        for g in range(GROUPS):
            here = [cotg.at[y, x, group(h, g), :] for h in (0, 1)]
            second[0, g] = [copy(here[0], here[0], x_dev(k)) for k in (1, 3, 2)]
            second[1, g] = [copy(here[1], here[1], y_dev(k)) for k in (1, 3, 2)]
        yield

    def gather_group(h, g):
        for c in second[h, g]:
            c.wait_recv()
        if h == 0:
            yield from gather_phase(lambda i, p: cotg.at[i, :, piece_of(h, g, p), :], y, y_dev)
        else:
            yield from gather_phase(lambda i, p: cotg.at[:, i, piece_of(h, g, p), :], x, x_dev)

    def gather_dots():
        for c in w_copies:
            c.wait()
        grad_dots(9, lambda k: (ring(y, 3 + lax.div(k, 3)), ring(x, 3 + lax.rem(k, 3))))
        yield
        grad_dots(
            7,
            lambda k: (
                ring(y, jnp.where(k < 4, 2, k - 1)),
                ring(x, jnp.where(k < 4, k, 2)),
            ),
        )
        gs[SECTIONS - 1] = acc[...].astype(BF16)
        yield

    diag = (
        lax.broadcasted_iota(jnp.int32, (COL, WIDTH), 0) // HALF
        == lax.rem(lax.broadcasted_iota(jnp.int32, (COL, WIDTH), 1), COL) // HALF
    )

    def spread(part):
        return jnp.where(diag, jnp.concatenate([part] * 4, axis=0), jnp.zeros((), BF16))

    def turned(ref, full):
        for lo, w in TILES:
            ref[lo : lo + w, 0:w] = full[0:w, lo : lo + w].T

    fac_copies = [None] * SECTIONS

    def setup():
        fac_copy.wait()
        for s in range(SECTIONS):
            fac_t[s] = jnp.concatenate([facv[s, j] for j in range(LANES)], axis=1)
        for s in reversed(range(SECTIONS)):
            fac_copies[s] = copy(fac_t.at[s, other_rows(s), :], fac_p.at[s], partner(s))
        for s in range(SECTIONS):
            own = spread(fac_t[s, own_rows(s), :])
            ma[s] = own
            turned(mat.at[s], own)
            turned(mbt.at[s], spread(fac_t[s, other_rows(s), :]))
        yield

    def span(part):
        lo = TILES[part[0]][0]
        return pl.ds(lo, TILES[part[-1]][0] + TILES[part[-1]][1] - lo)

    loaded = []

    def forward(part):
        if not loaded:
            hid_copy.wait()
            loaded.append(True)
        for s in range(SECTIONS):
            rows = span(part)
            c = copy(xs.at[s, rows, :], xp.at[s, rows, :], partner(s))
            yield
            c.wait_recv()
            for i in part:
                lo, w = TILES[i]
                own = xs[s, lo : lo + w, :]
                mix = dot(mat[s, lo : lo + w, 0:w], own)
                mix += dot(mbt[s, lo : lo + w, 0:w], xp[s, lo : lo + w, :])
                xs[s + 1, lo : lo + w, :] = (own.astype(F32) + mix).astype(BF16)
        yield

    def proj_dots(n, place):
        def step(k, carry):
            yy, xx = place(k)
            par[yy, xx] = dot(proj_in[0], wv[yy * SIDE + xx]).astype(BF16)
            return carry

        lax.fori_loop(0, n, step, 0)

    proj_in = [None]

    def add_to(ref, *others):
        total = ref[...].astype(F32)
        for o in others:
            total += o[...].astype(F32)
        ref[...] = total.astype(BF16)

    def sum_view(h, g):
        if h == 0:
            return lambda i, p: par.at[i, :, piece_of(h, g, p), :]
        return lambda i, p: par.at[:, i, piece_of(h, g, p), :]

    first = {(h, g): [] for h in (0, 1) for g in range(GROUPS)}

    def send_far(h):
        i, dev = ((y, y_dev), (x, x_dev))[h]
        for g in range(GROUPS):
            view = sum_view(h, g)
            first[h, g].append(copy(view(ring(i, 2), 0), buf1.at[h, g, 0], dev(1)))
            first[h, g].append(copy(view(ring(i, 2), 1), buf1.at[h, g, 1], dev(3)))

    def send_near(h):
        i, dev = ((y, y_dev), (x, x_dev))[h]
        for g in range(GROUPS):
            view = sum_view(h, g)
            first[h, g].append(copy(view(ring(i, 1), 1), buf2.at[h, g, 0, 1], dev(1)))
            first[h, g].append(copy(view(ring(i, 3), 0), buf2.at[h, g, 1, 0], dev(3)))

    def scatter():
        proj_in[0] = xs[SECTIONS].T
        proj_dots(4, lambda k: (ring(y, 2), ring(x, k)))
        send_far(0)
        yield
        proj_dots(3, lambda k: (ring(y, 3 + k), ring(x, 2)))
        send_far(1)
        yield
        proj_dots(6, lambda k: (ring(y, 1 + 2 * lax.div(k, 3)), ring(x, 3 + lax.rem(k, 3))))
        send_near(0)
        yield
        proj_dots(3, lambda k: (y, ring(x, 3 + k)))
        send_near(1)
        yield

    def scatter_group(h, g):
        view, rows = sum_view(h, g), group(h, g)
        i, dev, dev2 = ((y, y_dev, x_dev), (x, x_dev, y_dev))[h]
        a, b, c, d = first[h, g]
        a.wait_recv()
        add_to(view(ring(i, 1), 0), buf1.at[h, g, 0])
        e = copy(view(ring(i, 1), 0), buf2.at[h, g, 0, 0], dev(1))
        b.wait_recv()
        add_to(view(ring(i, 3), 1), buf1.at[h, g, 1])
        f = copy(view(ring(i, 3), 1), buf2.at[h, g, 1, 1], dev(3))
        yield
        c.wait_recv()
        f.wait_recv()
        add_to(view(i, 1), buf2.at[h, g, 0, 1], buf2.at[h, g, 1, 1])
        d.wait_recv()
        e.wait_recv()
        add_to(view(i, 0), buf2.at[h, g, 0, 0], buf2.at[h, g, 1, 0])
        copies = []
        for k in (2, 1, 3):
            src = par.at[y, ring(x, k), rows, :] if h == 0 else par.at[ring(y, k), x, rows, :]
            copies.append(copy(src, buf3.at[h, g, k - 1], dev2(k)))
        yield
        for c in copies:
            c.wait_recv()
        add_to(par.at[y, x, rows, :], *[buf3.at[h, g, k] for k in range(3)])
        copies = [
            copy(par.at[y, x, rows, columns(ring(z, k))], zr.at[h, g, k - 1], z_dev(k))
            for k in (1, 2, 3)
        ]
        yield
        total = par[y, x, rows, columns(z)].astype(F32)
        for k in (1, 2, 3):
            copies[k - 1].wait_recv()
            total += zr[h, g, k - 1].astype(F32)
        proj[rows, :] = total.astype(BF16)
        put(proj.at[rows, :], proj_out.at[rows, :])
        yield

    joined = []

    def backward(part):
        for s in reversed(range(SECTIONS)):
            rows = span(part)
            c = copy(gs.at[s, rows, :], gp.at[s, rows, :], partner(s))
            if s not in joined:
                fac_copies[s].wait_recv()
                mp[s] = spread(fac_p[s])
                joined.append(s)
            yield
            c.wait_recv()
            for i in part:
                lo, w = TILES[i]
                own = gs[s, lo : lo + w, :]
                back = dot(ma[s, 0:w, lo : lo + w], own)
                back += dot(mp[s, 0:w, lo : lo + w], gp[s, lo : lo + w, :])
                new = (own.astype(F32) + back).astype(BF16)
                if s == 0:
                    hgrad[lo : lo + w, :] = new
                else:
                    gs[s - 1, lo : lo + w, :] = new
        put(hgrad.at[rows, :], hgrad_out.at[rows, :])
        yield

    keep = pl.ds(pl.multiple_of(HALF * core, HALF), HALF)
    give = pl.ds(pl.multiple_of(HALF - HALF * core, HALF), HALF)

    def factor(s):
        for act, rows in ((xs.at[s], own_rows(s)), (xp.at[s], other_rows(s))):
            for lo, w in TILES:
                full = dot(act[lo : lo + w, :], gs[s, lo : lo + w, :], NT)
                full = jnp.where(diag[:w, :w], full, 0.0)
                total = full[0:HALF]
                for g in range(1, w // HALF):
                    total += full[g * HALF : (g + 1) * HALF]
                fg[s, rows, lo : lo + w] = total
        if s == 0:
            a = copy(fg.at[s], fg_all.at[s], core_dev)
            yield
            a.wait_recv()
            chip = (fg[s] + fg_all[s]).astype(BF16)
            fg_half[...] = chip
            b = copy(fg_half.at[keep, :], fg_far.at[s, keep, :], far_dev)
            c = copy(fg_half.at[keep, :], fg_far.at[s, keep, :], cross_dev)
            yield
            b.wait_recv()
            c.wait_recv()
            total = chip.astype(F32) + fg_far[s].astype(F32)
        else:
            a = copy(fg.at[s, give, :], fg_core.at[s], core_dev)
            yield
            a.wait_recv()
            chip = (fg[s, keep, :] + fg_core[s]).astype(BF16)
            fg_far[s, give, :] = chip
            b = copy(fg_far.at[s, give, :], fg_far.at[s, keep, :], far_dev)
            yield
            b.wait_recv()
            fg_all[s, keep, :] = chip.astype(F32) + fg_far[s, keep, :].astype(F32)
            c = copy(fg_all.at[s, keep, :], fg_all.at[s, keep, :], core_dev)
            yield
            c.wait_recv()
            total = fg_all[s]
        total = total * (1.0 / (4 * ROWS))
        for j in range(LANES):
            fgrad[s, j] = total[:, 2 * HALF * j : 2 * HALF * (j + 1)]
        put(fgrad.at[s], fgrad_out.at[s])
        yield

    chains = {"G": gather(), "GD": gather_dots(), "S": setup(), "R": scatter()}
    for g in range(GROUPS):
        for h, name in enumerate("AB"):
            chains[f"G{name}{g}"] = gather_group(h, g)
            chains[f"R{name}{g}"] = scatter_group(h, g)
    for n, part in enumerate(PARTS):
        chains[f"F{n}"] = forward(part)
        chains[f"B{n}"] = backward(part)
    for s in range(SECTIONS):
        chains[f"D{s}"] = factor(s)
    for name in sum(SCHEDULE, ()):
        next(chains[name], None)
    for chain in chains.values():
        for _ in chain:
            pass
    assert len(started) == COPIES
    for c in started:
        c.wait_send()
    for c in stored:
        c.wait()


COPIES = 3 + 6 + 18 + 12 * len(PARTS) + 2 * GROUPS * 21
STORES = 2 * GROUPS + len(PARTS) + SECTIONS


def body(hidden, weight, factors, cotangent):
    anywhere = pl.BlockSpec(memory_space=pl.ANY)
    part = (SIDE, CHUNK // GROUPS // 2, BLOCK)
    acts = (SECTIONS, WIDTH, ROWS)
    scratch = [
        ((SIDE * SIDE, WIDTH, BLOCK), BF16),
        ((ROWS, COL), BF16),
        ((SECTIONS, LANES, 2 * HALF, 2 * HALF), BF16),
        ((SIDE, SIDE, ROWS, BLOCK), BF16),
        ((SIDE, SIDE, ROWS, BLOCK), BF16),
        ((SECTIONS + 1, WIDTH, ROWS), BF16),
        (acts, BF16),
        (acts, BF16),
        (acts, BF16),
        ((SECTIONS, 2 * HALF, WIDTH), BF16),
        ((SECTIONS, HALF, WIDTH), BF16),
        ((SECTIONS, COL, WIDTH), BF16),
        ((SECTIONS, WIDTH, COL), BF16),
        ((SECTIONS, WIDTH, COL), BF16),
        ((SECTIONS, COL, WIDTH), BF16),
        ((SECTIONS, 2 * HALF, WIDTH), F32),
        ((SECTIONS, HALF, WIDTH), F32),
        ((2 * HALF, WIDTH), BF16),
        ((SECTIONS, 2 * HALF, WIDTH), BF16),
        ((SECTIONS, 2 * HALF, WIDTH), F32),
        ((WIDTH, ROWS), F32),
        ((2, GROUPS, 2) + part, BF16),
        ((2, GROUPS, 2, 2) + part, BF16),
        ((2, GROUPS, 3, CHUNK // GROUPS, BLOCK), BF16),
        ((2, GROUPS, 3, CHUNK // GROUPS, COL), BF16),
        ((ROWS, COL), BF16),
        ((WIDTH, ROWS), BF16),
        ((SECTIONS, LANES, 2 * HALF, 2 * HALF), F32),
    ]
    proj, hgrad, fgrad = pl.pallas_call(
        kernel,
        out_shape=(
            jax.ShapeDtypeStruct((ROWS, COL), BF16),
            jax.ShapeDtypeStruct((WIDTH, ROWS), BF16),
            jax.ShapeDtypeStruct((SECTIONS, LANES, 2 * HALF, 2 * HALF), F32),
        ),
        in_specs=[anywhere] * 4,
        out_specs=(anywhere,) * 3,
        scratch_shapes=[pltpu.VMEM(*one) for one in scratch]
        + [
            pltpu.SemaphoreType.DMA((3 + SIDE * SIDE,)),
            pltpu.SemaphoreType.DMA((STORES,)),
            pltpu.SemaphoreType.DMA((COPIES,)),
            pltpu.SemaphoreType.DMA((COPIES,)),
        ],
        compiler_params=pltpu.CompilerParams(
            collective_id=0, has_side_effects=True, vmem_limit_bytes=56 * 1024 * 1024
        ),
        name="butterfly",
    )(hidden.T, weight, factors, cotangent)
    return proj, hgrad.T, fgrad


def solution(mesh):
    return jax.shard_map(
        body,
        mesh=mesh,
        in_specs=(
            P("dp", "tensor"),
            P("tensor", None),
            P(None, "tensor", None, None),
            P("dp", "tensor"),
        ),
        out_specs=(P("dp", "tensor"), P("dp", "tensor"), P(None, "tensor", None, None)),
        check_vma=False,
    )
```

```python
import jax
import jax.numpy as jnp
from jax import lax
from jax.experimental import pallas as pl
from jax.experimental.pallas import tpu as pltpu
from jax.sharding import PartitionSpec as P

MESH = pl.DeviceIdType.MESH
BF16 = jnp.bfloat16
F32 = jnp.float32

ROWS = 256
WIDTH = 448
LANES = 7
HALF = 32
SECTIONS = 6
SIDE = 4
COL = 128
BLOCK = SIDE * COL
HALVES = 2
TOKENS = ROWS // HALVES
GROUP = TOKENS // 2
PIECE = GROUP // 2
TILES = ((0, 128), (128, 128), (256, 128), (384, 64))
SPLIT = ((0,), (1,), (2, 3))
PARTS = tuple((tiles, half) for half in range(HALVES) for tiles in SPLIT)
GROUPS = tuple((half, first) for half in range(HALVES) for first in (0, 1))

SCHEDULE = (
    ("G0", "F0", "G1", "G2", "S", "G0", "F2", "G1", "G3", "F5", "G2", "F0"),
    ("G0", "G1", "F0", "G3", "F3", "F2", "G1", "F5", "F1", "F2", "F4", "G0"),
    ("G2", "G0", "F4", "G1", "G3", "F3", "N0", "G1", "F2", "F0", "F1", "G2"),
    ("G0", "F4", "N0", "B2", "G2", "G3", "G3", "B1", "B0", "F1", "F2", "F0"),
    ("N1", "B1", "B0", "G3", "G2", "F3", "F5", "B2", "F1", "F2", "N1", "B4"),
    ("B3", "B1", "B5", "F4", "F5", "F0", "F3", "B2", "B4", "B1", "B0", "B3"),
    ("F1", "B5", "F0", "F5", "B4", "F2", "B3", "B2", "F1", "B5", "F3", "F4"),
    ("B3", "B4", "B0", "F5", "F1", "R0", "B1", "B2", "B5", "F3", "F4", "R0"),
    ("R0", "D2", "R0", "B0", "D3", "B1", "B5", "F5", "B4", "F4", "Q1", "Q0"),
    ("F3", "B3", "R1", "R1", "D2", "R1", "D4", "B5", "D5", "D3", "R1", "B2"),
    ("D5", "B4", "B3", "B0", "Q2", "D4", "B5", "D1", "Q3", "D0", "Q1", "D0"),
    ("Q0", "D3", "D2", "Q3", "Q2", "D1", "Q1", "D2", "Q0", "D4", "B3", "D0"),
    ("Q3", "D4", "D5", "Q1", "D1", "D3", "Q2", "D5", "B4", "B0", "Q3", "B2"),
    ("D1", "B1", "Q0", "Q2"),
)


def dot(a, b, contract=((1,), (0,))):
    return lax.dot_general(a, b, (contract, ((), ())), preferred_element_type=F32)


NT = ((1,), (1,))


def kernel(
    hid, w_hbm, fac_hbm, cot_hbm, proj_out, hgrad_out, fgrad_out,
    wv, cotv, facv, cotg, par, xs, xp, gs, gp, fac_t, fac_p, ma, mat, mbt, mp,
    fg, fg_core, fg_half, fg_far, fg_all, acc, buf1, buf2, buf3, zr,
    proj, hgrad, fgrad, in_sem, out_sem, send, recv,
):
    dp = lax.axis_index("dp")
    t = lax.axis_index("tensor")
    y = lax.div(t, SIDE * SIDE)
    x = lax.rem(lax.div(t, SIDE), SIDE)
    z = lax.rem(t, SIDE)
    core = lax.rem(dp, 2)

    def ring(v, k):
        return lax.rem(v + k, SIDE)

    def at(yy, xx, zz):
        return (dp, (yy * SIDE + xx) * SIDE + zz)

    def y_dev(k):
        return at(ring(y, k), x, z)

    def x_dev(k):
        return at(y, ring(x, k), z)

    def z_dev(k):
        return at(y, x, ring(z, k))

    far = lax.rem(dp + 2, 4)
    core_dev = (dp + 1 - 2 * core, t)
    far_dev = (far, t)
    cross_dev = (far + 1 - 2 * core, t)

    def bit_of(s):
        return lax.rem(lax.div(t, 1 << s), 2)

    def partner(s):
        return (dp, t + (1 << s) * (1 - 2 * bit_of(s)))

    def own_rows(s):
        return pl.ds(pl.multiple_of(HALF * bit_of(s), HALF), HALF)

    def other_rows(s):
        return pl.ds(pl.multiple_of(HALF - HALF * bit_of(s), HALF), HALF)

    started = []

    def copy(src, dst, dev):
        k = len(started)
        c = pltpu.make_async_remote_copy(
            src_ref=src, dst_ref=dst, send_sem=send.at[k], recv_sem=recv.at[k],
            device_id=dev, device_id_type=MESH,
        )
        c.start()
        started.append(c)
        return c

    def fetch(src, dst, k):
        c = pltpu.make_async_copy(src, dst, in_sem.at[k])
        c.start()
        return c

    cot_copy = fetch(cot_hbm, cotv, 0)
    hid_copy = fetch(hid, xs.at[0], 1)
    fac_copy = fetch(fac_hbm, facv, 2)
    w_copies = [
        fetch(w_hbm.at[:, pl.ds(b * BLOCK, BLOCK)], wv.at[b], 3 + b) for b in range(SIDE * SIDE)
    ]
    stored = []

    def put(src, dst):
        c = pltpu.make_async_copy(src, dst, out_sem.at[len(stored)])
        c.start()
        stored.append(c)

    peers = [f(k) for f in (z_dev, x_dev, y_dev) for k in (1, 2, 3)]
    peers += [core_dev, far_dev, cross_dev]
    barrier = pltpu.get_barrier_semaphore()
    for dev in peers:
        pl.semaphore_signal(barrier, inc=1, device_id=dev, device_id_type=MESH)
    pl.semaphore_wait(barrier, len(peers))

    def start_of(i):
        half, first = GROUPS[i]
        return TOKENS * half + GROUP * first

    def group(i):
        return pl.ds(start_of(i), GROUP)

    def piece(i, p):
        return pl.ds(start_of(i) + PIECE * p, PIECE)

    def tokens(half):
        return pl.ds(TOKENS * half, TOKENS)

    def gather_phase(view, i, dev):
        r1 = copy(view(i, 0), view(i, 0), dev(1))
        l2 = copy(view(i, 1), view(i, 1), dev(3))
        r2 = copy(view(i, 1), view(i, 1), dev(1))
        l1 = copy(view(i, 0), view(i, 0), dev(3))
        yield
        left, right = ring(i, 3), ring(i, 1)
        r1.wait_recv()
        far1 = copy(view(left, 0), view(left, 0), dev(1))
        l2.wait_recv()
        far2 = copy(view(right, 1), view(right, 1), dev(3))
        yield
        r2.wait_recv()
        l1.wait_recv()
        yield
        far1.wait_recv()
        far2.wait_recv()
        yield

    def grad_dots(half, n, place):
        def step(k, carry):
            yy, xx = place(k)
            acc[half] += dot(wv[yy * SIDE + xx], cotg[yy, xx, tokens(half), :], NT)
            return carry

        lax.fori_loop(0, n, step, 0)

    def columns(zz):
        return pl.ds(pl.multiple_of(zz * COL, COL), COL)

    loaded = []

    def once(c):
        if all(c is not d for d in loaded):
            c.wait()
            loaded.append(c)

    def gather(i):
        once(cot_copy)
        first = GROUPS[i][1]
        dev, dev2, n = ((x_dev, y_dev, y), (y_dev, x_dev, x))[first]
        rows = group(i)
        mine = cotg.at[y, x, rows, columns(z)]
        copies = [copy(cotv.at[rows, :], mine, z_dev(k)) for k in (1, 2, 3)]
        mine[...] = cotv[rows, :]
        yield
        for c in copies:
            c.wait_recv()
        here = cotg.at[y, x, rows, :]
        copies = [copy(here, here, dev(k)) for k in (1, 3, 2)]
        yield
        for c in copies:
            c.wait_recv()
        if first == 0:
            yield from gather_phase(lambda j, p: cotg.at[j, :, piece(i, p), :], n, dev2)
        else:
            yield from gather_phase(lambda j, p: cotg.at[:, j, piece(i, p), :], n, dev2)

    def gather_dots(half):
        for c in w_copies:
            once(c)
        acc[half] = jnp.zeros((WIDTH, TOKENS), F32)
        grad_dots(half, 9, lambda k: (ring(y, 3 + lax.div(k, 3)), ring(x, 3 + lax.rem(k, 3))))
        yield
        grad_dots(
            half,
            7,
            lambda k: (
                ring(y, jnp.where(k < 4, 2, k - 1)),
                ring(x, jnp.where(k < 4, k, 2)),
            ),
        )
        gs[SECTIONS - 1, :, tokens(half)] = acc[half].astype(BF16)
        yield

    diag = (
        lax.broadcasted_iota(jnp.int32, (COL, WIDTH), 0) // HALF
        == lax.rem(lax.broadcasted_iota(jnp.int32, (COL, WIDTH), 1), COL) // HALF
    )

    def spread(part):
        return jnp.where(diag, jnp.concatenate([part] * 4, axis=0), jnp.zeros((), BF16))

    def turned(ref, full):
        for lo, w in TILES:
            ref[lo : lo + w, 0:w] = full[0:w, lo : lo + w].T

    fac_copies = [None] * SECTIONS

    def setup():
        fac_copy.wait()
        for s in range(SECTIONS):
            fac_t[s] = jnp.concatenate([facv[s, j] for j in range(LANES)], axis=1)
        for s in reversed(range(SECTIONS)):
            fac_copies[s] = copy(fac_t.at[s, other_rows(s), :], fac_p.at[s], partner(s))
        for s in range(SECTIONS):
            own = spread(fac_t[s, own_rows(s), :])
            ma[s] = own
            turned(mat.at[s], own)
            turned(mbt.at[s], spread(fac_t[s, other_rows(s), :]))
        yield

    def span(tiles):
        lo = TILES[tiles[0]][0]
        return pl.ds(lo, TILES[tiles[-1]][0] + TILES[tiles[-1]][1] - lo)

    def forward(tiles, half):
        once(hid_copy)
        rows, cols = span(tiles), tokens(half)
        for s in range(SECTIONS):
            c = copy(xs.at[s, rows, cols], xp.at[s, rows, cols], partner(s))
            yield
            c.wait_recv()
            for i in tiles:
                lo, w = TILES[i]
                own = xs[s, lo : lo + w, cols]
                mix = dot(mat[s, lo : lo + w, 0:w], own)
                mix += dot(mbt[s, lo : lo + w, 0:w], xp[s, lo : lo + w, cols])
                xs[s + 1, lo : lo + w, cols] = (own.astype(F32) + mix).astype(BF16)
        yield

    def proj_dots(half, left, n, place):
        def step(k, carry):
            yy, xx = place(k)
            par[yy, xx, tokens(half), :] = dot(left, wv[yy * SIDE + xx]).astype(BF16)
            return carry

        lax.fori_loop(0, n, step, 0)

    def add_to(ref, *others):
        total = ref[...].astype(F32)
        for o in others:
            total += o[...].astype(F32)
        ref[...] = total.astype(BF16)

    def sum_view(i):
        if GROUPS[i][1] == 0:
            return lambda j, p: par.at[j, :, piece(i, p), :]
        return lambda j, p: par.at[:, j, piece(i, p), :]

    early = {i: [] for i in range(len(GROUPS))}

    def send_far(i):
        n, dev = ((y, y_dev), (x, x_dev))[GROUPS[i][1]]
        view = sum_view(i)
        early[i].append(copy(view(ring(n, 2), 0), buf1.at[i, 0], dev(1)))
        early[i].append(copy(view(ring(n, 2), 1), buf1.at[i, 1], dev(3)))

    def send_near(i):
        n, dev = ((y, y_dev), (x, x_dev))[GROUPS[i][1]]
        view = sum_view(i)
        early[i].append(copy(view(ring(n, 1), 1), buf2.at[i, 0, 1], dev(1)))
        early[i].append(copy(view(ring(n, 3), 0), buf2.at[i, 1, 0], dev(3)))

    def scatter(half):
        for c in w_copies:
            once(c)
        left = xs[SECTIONS, :, tokens(half)].T
        a, b = GROUPS.index((half, 0)), GROUPS.index((half, 1))
        proj_dots(half, left, 4, lambda k: (ring(y, 2), ring(x, k)))
        send_far(a)
        yield
        proj_dots(half, left, 3, lambda k: (ring(y, 3 + k), ring(x, 2)))
        send_far(b)
        yield
        proj_dots(
            half, left, 6,
            lambda k: (ring(y, 1 + 2 * lax.div(k, 3)), ring(x, 3 + lax.rem(k, 3))),
        )
        send_near(a)
        yield
        proj_dots(half, left, 3, lambda k: (y, ring(x, 3 + k)))
        send_near(b)
        yield

    def scatter_group(i):
        view, rows = sum_view(i), group(i)
        first = GROUPS[i][1]
        n, dev, dev2 = ((y, y_dev, x_dev), (x, x_dev, y_dev))[first]
        a, b, c, d = early[i]
        a.wait_recv()
        add_to(view(ring(n, 1), 0), buf1.at[i, 0])
        e = copy(view(ring(n, 1), 0), buf2.at[i, 0, 0], dev(1))
        b.wait_recv()
        add_to(view(ring(n, 3), 1), buf1.at[i, 1])
        f = copy(view(ring(n, 3), 1), buf2.at[i, 1, 1], dev(3))
        yield
        c.wait_recv()
        f.wait_recv()
        add_to(view(n, 1), buf2.at[i, 0, 1], buf2.at[i, 1, 1])
        d.wait_recv()
        e.wait_recv()
        add_to(view(n, 0), buf2.at[i, 0, 0], buf2.at[i, 1, 0])
        copies = []
        for k in (2, 1, 3):
            src = par.at[y, ring(x, k), rows, :] if first == 0 else par.at[ring(y, k), x, rows, :]
            copies.append(copy(src, buf3.at[i, k - 1], dev2(k)))
        yield
        for c in copies:
            c.wait_recv()
        add_to(par.at[y, x, rows, :], *[buf3.at[i, k] for k in range(3)])
        copies = [
            copy(par.at[y, x, rows, columns(ring(z, k))], zr.at[i, k - 1], z_dev(k))
            for k in (1, 2, 3)
        ]
        yield
        total = par[y, x, rows, columns(z)].astype(F32)
        for k in (1, 2, 3):
            copies[k - 1].wait_recv()
            total += zr[i, k - 1].astype(F32)
        proj[rows, :] = total.astype(BF16)
        put(proj.at[rows, :], proj_out.at[rows, :])
        yield

    joined = []

    def backward(tiles, half):
        rows, cols = span(tiles), tokens(half)
        for s in reversed(range(SECTIONS)):
            c = copy(gs.at[s, rows, cols], gp.at[s, rows, cols], partner(s))
            if s not in joined:
                fac_copies[s].wait_recv()
                mp[s] = spread(fac_p[s])
                joined.append(s)
            yield
            c.wait_recv()
            for i in tiles:
                lo, w = TILES[i]
                own = gs[s, lo : lo + w, cols]
                back = dot(ma[s, 0:w, lo : lo + w], own)
                back += dot(mp[s, 0:w, lo : lo + w], gp[s, lo : lo + w, cols])
                new = (own.astype(F32) + back).astype(BF16)
                if s == 0:
                    hgrad[lo : lo + w, cols] = new
                else:
                    gs[s - 1, lo : lo + w, cols] = new
        put(hgrad.at[rows, cols], hgrad_out.at[rows, cols])
        yield

    keep = pl.ds(pl.multiple_of(HALF * core, HALF), HALF)
    give = pl.ds(pl.multiple_of(HALF - HALF * core, HALF), HALF)

    def factor(s):
        for act, rows in ((xs.at[s], own_rows(s)), (xp.at[s], other_rows(s))):
            for lo, w in TILES:
                full = dot(act[lo : lo + w, :], gs[s, lo : lo + w, :], NT)
                full = jnp.where(diag[:w, :w], full, 0.0)
                total = full[0:HALF]
                for g in range(1, w // HALF):
                    total += full[g * HALF : (g + 1) * HALF]
                fg[s, rows, lo : lo + w] = total
        if s == 0:
            a = copy(fg.at[s], fg_all.at[s], core_dev)
            yield
            a.wait_recv()
            chip = (fg[s] + fg_all[s]).astype(BF16)
            fg_half[...] = chip
            b = copy(fg_half.at[keep, :], fg_far.at[s, keep, :], far_dev)
            c = copy(fg_half.at[keep, :], fg_far.at[s, keep, :], cross_dev)
            yield
            b.wait_recv()
            c.wait_recv()
            total = chip.astype(F32) + fg_far[s].astype(F32)
        else:
            a = copy(fg.at[s, give, :], fg_core.at[s], core_dev)
            yield
            a.wait_recv()
            chip = (fg[s, keep, :] + fg_core[s]).astype(BF16)
            fg_far[s, give, :] = chip
            b = copy(fg_far.at[s, give, :], fg_far.at[s, keep, :], far_dev)
            yield
            b.wait_recv()
            fg_all[s, keep, :] = chip.astype(F32) + fg_far[s, keep, :].astype(F32)
            c = copy(fg_all.at[s, keep, :], fg_all.at[s, keep, :], core_dev)
            yield
            c.wait_recv()
            total = fg_all[s]
        total = total * (1.0 / (4 * ROWS))
        for j in range(LANES):
            fgrad[s, j] = total[:, 2 * HALF * j : 2 * HALF * (j + 1)]
        put(fgrad.at[s], fgrad_out.at[s])
        yield

    chains = {"S": setup()}
    for half in range(HALVES):
        chains[f"N{half}"] = gather_dots(half)
        chains[f"R{half}"] = scatter(half)
    for i in range(len(GROUPS)):
        chains[f"G{i}"] = gather(i)
        chains[f"Q{i}"] = scatter_group(i)
    for i, part in enumerate(PARTS):
        chains[f"F{i}"] = forward(*part)
        chains[f"B{i}"] = backward(*part)
    for s in range(SECTIONS):
        chains[f"D{s}"] = factor(s)
    for name in sum(SCHEDULE, ()):
        next(chains[name], None)
    for chain in chains.values():
        for _ in chain:
            pass
    assert len(started) == COPIES
    for c in started:
        c.wait_send()
    for c in stored:
        c.wait()


COPIES = 6 + 18 + 12 * len(PARTS) + 24 * len(GROUPS)
STORES = len(GROUPS) + len(PARTS) + SECTIONS


def hand_on(*refs):
    for i in range(3):
        refs[3 + i][...] = refs[i][...]


def body(hidden, weight, factors, cotangent):
    anywhere = pl.BlockSpec(memory_space=pl.ANY)
    groups, part = len(GROUPS), (SIDE, PIECE, BLOCK)
    acts = (SECTIONS, WIDTH, ROWS)
    scratch = [
        ((SIDE * SIDE, WIDTH, BLOCK), BF16),
        ((ROWS, COL), BF16),
        ((SECTIONS, LANES, 2 * HALF, 2 * HALF), BF16),
        ((SIDE, SIDE, ROWS, BLOCK), BF16),
        ((SIDE, SIDE, ROWS, BLOCK), BF16),
        ((SECTIONS + 1, WIDTH, ROWS), BF16),
        (acts, BF16),
        (acts, BF16),
        (acts, BF16),
        ((SECTIONS, 2 * HALF, WIDTH), BF16),
        ((SECTIONS, HALF, WIDTH), BF16),
        ((SECTIONS, COL, WIDTH), BF16),
        ((SECTIONS, WIDTH, COL), BF16),
        ((SECTIONS, WIDTH, COL), BF16),
        ((SECTIONS, COL, WIDTH), BF16),
        ((SECTIONS, 2 * HALF, WIDTH), F32),
        ((SECTIONS, HALF, WIDTH), F32),
        ((2 * HALF, WIDTH), BF16),
        ((SECTIONS, 2 * HALF, WIDTH), BF16),
        ((SECTIONS, 2 * HALF, WIDTH), F32),
        ((HALVES, WIDTH, TOKENS), F32),
        ((groups, 2) + part, BF16),
        ((groups, 2, 2) + part, BF16),
        ((groups, 3, GROUP, BLOCK), BF16),
        ((groups, 3, GROUP, COL), BF16),
        ((ROWS, COL), BF16),
        ((WIDTH, ROWS), BF16),
        ((SECTIONS, LANES, 2 * HALF, 2 * HALF), F32),
    ]
    proj, hgrad, fgrad = pl.pallas_call(
        kernel,
        out_shape=(
            jax.ShapeDtypeStruct((ROWS, COL), BF16),
            jax.ShapeDtypeStruct((WIDTH, ROWS), BF16),
            jax.ShapeDtypeStruct((SECTIONS, LANES, 2 * HALF, 2 * HALF), F32),
        ),
        in_specs=[anywhere] * 4,
        out_specs=(anywhere,) * 3,
        scratch_shapes=[pltpu.VMEM(*one) for one in scratch]
        + [
            pltpu.SemaphoreType.DMA((3 + SIDE * SIDE,)),
            pltpu.SemaphoreType.DMA((STORES,)),
            pltpu.SemaphoreType.DMA((COPIES,)),
            pltpu.SemaphoreType.DMA((COPIES,)),
        ],
        compiler_params=pltpu.CompilerParams(
            collective_id=0, has_side_effects=True, vmem_limit_bytes=56 * 1024 * 1024
        ),
        name="butterfly",
    )(hidden.T, weight, factors, cotangent)
    outs = (proj, hgrad, fgrad)
    proj, hgrad, fgrad = pl.pallas_call(
        hand_on,
        out_shape=tuple(jax.ShapeDtypeStruct(o.shape, o.dtype) for o in outs),
        in_specs=[pl.BlockSpec(memory_space=pltpu.VMEM)] * 3,
        out_specs=(pl.BlockSpec(memory_space=pltpu.VMEM),) * 3,
        name="hand_on",
    )(*outs)
    return proj, hgrad.T, fgrad


def solution(mesh):
    return jax.shard_map(
        body,
        mesh=mesh,
        in_specs=(
            P("dp", "tensor"),
            P("tensor", None),
            P(None, "tensor", None, None),
            P("dp", "tensor"),
        ),
        out_specs=(P("dp", "tensor"), P("dp", "tensor"), P(None, "tensor", None, None)),
        check_vma=False,
    )
```

```python
import jax
import jax.numpy as jnp
from jax import lax
from jax.experimental import pallas as pl
from jax.experimental.pallas import tpu as pltpu
from jax.sharding import PartitionSpec as P

MESH = pl.DeviceIdType.MESH
BF16 = jnp.bfloat16
F32 = jnp.float32

ROWS = 256
WIDTH = 448
LANES = 7
HALF = 32
SECTIONS = 6
SIDE = 4
COL = 128
BLOCK = SIDE * COL
HALVES = 2
TOKENS = ROWS // HALVES
GROUP = TOKENS // 2
SLACK = GROUP // 2
TILES = ((0, 128), (128, 128), (256, 128), (384, 64))
SPLIT = ((0,), (1,), (2, 3))
PARTS = tuple((tiles, half) for half in range(HALVES) for tiles in SPLIT)
GROUPS = tuple((half, first) for half in range(HALVES) for first in (0, 1))

BATCHES = ((5, 4, 3), (2, 1), (0,))

SCHEDULE = (
    ("F2", "G2", "G3", "G0", "G1", "F2", "S", "G2", "G3", "G0", "G1", "F1"),
    ("F2", "G2", "G3", "F4", "F0", "F5", "F0", "F5", "F2", "G2", "F1", "G3"),
    ("G0", "F0", "F3", "G1", "G3", "G2", "N1", "F2", "G3", "F0", "G2", "N1"),
    ("B3", "F1", "B5", "H", "F4", "G1", "G0", "F3", "B4", "G0", "F2", "G1"),
    ("F5", "N0", "F1", "B3", "F0", "B5", "F3", "H", "G0", "G1", "N0", "B2"),
    ("F4", "F5", "B0", "F1", "B1", "F3", "F2", "B3", "F0", "B4", "F4", "H"),
    ("B5", "F1", "B2", "F5", "B4", "B0", "B3", "B1", "F0", "F3", "F4", "B5"),
    ("F1", "B2", "R0", "H", "B4", "B0", "B1", "F5", "E3", "B3", "B5", "R0"),
    ("F4", "F3", "R0", "B0", "E4", "B2", "B1", "H", "B4", "R0", "F5", "F4"),
    ("F3", "R1", "R1", "B2", "R1", "B0", "Q1", "B1", "B3", "E5", "B5", "D0"),
    ("Q2", "R1", "B4", "B0", "Q0", "D0", "B2", "Q3", "B1", "E1", "E0", "B3"),
    ("D2", "E2", "D1", "Q1", "D1", "D2", "Q2", "Q3", "B1", "Q0", "D0", "B2"),
    ("Q1", "Q2", "Q3", "B4", "Q0", "D1", "B0", "Q1", "B5", "D1", "D0", "Q2"),
    ("Q3", "D2", "Q0"),
)


def dot(a, b, contract=((1,), (0,))):
    return lax.dot_general(a, b, (contract, ((), ())), preferred_element_type=F32)


NT = ((1,), (1,))


def kernel(
    hid, w_hbm, fac_hbm, cot_hbm, proj_out, hgrad_out, fgrad_out,
    wv, cotv, facv, cotg, par, xs, xp, gs, gp, fac_t, fac_p, ma, mat, mbt, mp,
    fg, fg_core, fg_half, fg_far, fg_all, acc, buf1, buf2, buf3, zr,
    proj, hgrad, fgrad, in_sem, out_sem, word, send, recv,
):
    dp = lax.axis_index("dp")
    t = lax.axis_index("tensor")
    y = lax.div(t, SIDE * SIDE)
    x = lax.rem(lax.div(t, SIDE), SIDE)
    z = lax.rem(t, SIDE)
    core = lax.rem(dp, 2)

    def ring(v, k):
        return lax.rem(v + k, SIDE)

    def at(yy, xx, zz):
        return (dp, (yy * SIDE + xx) * SIDE + zz)

    def y_dev(k):
        return at(ring(y, k), x, z)

    def x_dev(k):
        return at(y, ring(x, k), z)

    def z_dev(k):
        return at(y, x, ring(z, k))

    far = lax.rem(dp + 2, 4)
    core_dev = (dp + 1 - 2 * core, t)
    far_dev = (far, t)
    cross_dev = (far + 1 - 2 * core, t)

    def bit_of(s):
        return lax.rem(lax.div(t, 1 << s), 2)

    def partner(s):
        return (dp, t + (1 << s) * (1 - 2 * bit_of(s)))

    def own_rows(s):
        return pl.ds(pl.multiple_of(HALF * bit_of(s), HALF), HALF)

    def other_rows(s):
        return pl.ds(pl.multiple_of(HALF - HALF * bit_of(s), HALF), HALF)

    started = []

    def copy(src, dst, dev):
        k = len(started)
        c = pltpu.make_async_remote_copy(
            src_ref=src, dst_ref=dst, send_sem=send.at[k], recv_sem=recv.at[k],
            device_id=dev, device_id_type=MESH,
        )
        c.start()
        started.append(c)
        return c

    def fetch(src, dst, k):
        c = pltpu.make_async_copy(src, dst, in_sem.at[k])
        c.start()
        return c

    cot_copy = fetch(cot_hbm, cotv, 0)
    hid_copy = fetch(hid, xs.at[0], 1)
    fac_copy = fetch(fac_hbm, facv, 2)
    w_copies = [
        fetch(w_hbm.at[:, pl.ds(b * BLOCK, BLOCK)], wv.at[b], 3 + b) for b in range(SIDE * SIDE)
    ]
    stored = []

    def put(src, dst):
        c = pltpu.make_async_copy(src, dst, out_sem.at[len(stored)])
        c.start()
        stored.append(c)

    peers = [f(k) for f in (z_dev, x_dev, y_dev) for k in (1, 2, 3)]
    run = lax.div(dp, 2) * SIDE + z

    def run_dev(k):
        to = lax.rem(run + k, 2 * SIDE)
        return (lax.div(to, SIDE) * 2 + core, t - z + lax.rem(to, SIDE))

    ends = [run_dev(1), run_dev(2 * SIDE - 1)]
    peers += [core_dev] + ends
    barrier = pltpu.get_barrier_semaphore()
    for dev in peers:
        pl.semaphore_signal(barrier, inc=1, device_id=dev, device_id_type=MESH)
    diag = (
        lax.broadcasted_iota(jnp.int32, (COL, WIDTH), 0) // HALF
        == lax.rem(lax.broadcasted_iota(jnp.int32, (COL, WIDTH), 1), COL) // HALF
    )

    def spread(part):
        return jnp.where(diag, jnp.concatenate([part] * 4, axis=0), jnp.zeros((), BF16))

    def turned(ref, full):
        for lo, w in TILES:
            ref[lo : lo + w, 0:w] = full[0:w, lo : lo + w].T

    fac_copy.wait()
    for s in range(SECTIONS):
        fac_t[s] = jnp.concatenate([facv[s, j] for j in range(LANES)], axis=1)
        own = spread(fac_t[s, own_rows(s), :])
        ma[s] = own
        turned(mat.at[s], own)
        turned(mbt.at[s], spread(fac_t[s, other_rows(s), :]))
    cot_copy.wait()
    hid_copy.wait()
    pl.semaphore_wait(barrier, len(peers))

    def start_of(i):
        half, first = GROUPS[i]
        return TOKENS * half + GROUP * first

    def group(i):
        return pl.ds(start_of(i), GROUP)

    pieces = ((0, SLACK), (SLACK, GROUP - SLACK))

    def piece(i, p):
        return pl.ds(start_of(i) + pieces[p][0], pieces[p][1])

    def bound(v):
        return 1 + 2 * lax.rem(v, 2), 3 - 2 * lax.rem(v, 2)

    def tokens(half):
        return pl.ds(TOKENS * half, TOKENS)

    def gather_phase(view, i, dev):
        near, other = bound(i)
        r1 = copy(view(i, 0), view(i, 0), dev(near))
        l2 = copy(view(i, 1), view(i, 1), dev(other))
        r2 = copy(view(i, 1), view(i, 1), dev(near))
        l1 = copy(view(i, 0), view(i, 0), dev(other))
        yield
        r1.wait_recv()
        there = view(ring(i, near), 0)
        far1 = copy(there, there, dev(other))
        l2.wait_recv()
        there = view(ring(i, other), 1)
        far2 = copy(there, there, dev(near))
        yield
        r2.wait_recv()
        l1.wait_recv()
        yield
        far1.wait_recv()
        far2.wait_recv()
        yield

    def grad_dots(half, n, place):
        def step(k, carry):
            yy, xx = place(k)
            acc[half] += dot(wv[yy * SIDE + xx], cotg[yy, xx, tokens(half), :], NT)
            return carry

        lax.fori_loop(0, n, step, 0)

    def columns(zz):
        return pl.ds(pl.multiple_of(zz * COL, COL), COL)

    loaded = []

    def once(c):
        if all(c is not d for d in loaded):
            c.wait()
            loaded.append(c)

    def gather(i):
        first = GROUPS[i][1]
        dev, dev2, n = ((x_dev, y_dev, y), (y_dev, x_dev, x))[first]
        rows = group(i)
        mine = cotg.at[y, x, rows, columns(z)]
        copies = [copy(cotv.at[rows, :], mine, z_dev(k)) for k in (1, 2, 3)]
        mine[...] = cotv[rows, :]
        yield
        for c in copies:
            c.wait_recv()
        here = cotg.at[y, x, rows, :]
        copies = [copy(here, here, dev(k)) for k in (1, 3, 2)]
        yield
        for c in copies:
            c.wait_recv()
        if first == 0:
            yield from gather_phase(lambda j, p: cotg.at[j, :, piece(i, p), :], n, dev2)
        else:
            yield from gather_phase(lambda j, p: cotg.at[:, j, piece(i, p), :], n, dev2)

    def gather_dots(half):
        for c in w_copies:
            once(c)
        acc[half] = jnp.zeros((WIDTH, TOKENS), F32)
        grad_dots(half, 9, lambda k: (ring(y, 3 + lax.div(k, 3)), ring(x, 3 + lax.rem(k, 3))))
        yield
        grad_dots(
            half,
            7,
            lambda k: (
                ring(y, jnp.where(k < 4, 2, k - 1)),
                ring(x, jnp.where(k < 4, k, 2)),
            ),
        )
        gs[SECTIONS - 1, :, tokens(half)] = acc[half].astype(BF16)
        yield

    fac_copies = [None] * SECTIONS

    def setup():
        for s in reversed(range(SECTIONS)):
            fac_copies[s] = copy(fac_t.at[s, other_rows(s), :], fac_p.at[s], partner(s))
        yield

    def span(tiles):
        lo = TILES[tiles[0]][0]
        return pl.ds(lo, TILES[tiles[-1]][0] + TILES[tiles[-1]][1] - lo)

    def forward(tiles, half):
        rows, cols = span(tiles), tokens(half)
        for s in range(SECTIONS):
            c = copy(xs.at[s, rows, cols], xp.at[s, rows, cols], partner(s))
            yield
            c.wait_recv()
            for i in tiles:
                lo, w = TILES[i]
                own = xs[s, lo : lo + w, cols]
                mix = dot(mat[s, lo : lo + w, 0:w], own)
                mix += dot(mbt[s, lo : lo + w, 0:w], xp[s, lo : lo + w, cols])
                xs[s + 1, lo : lo + w, cols] = (own.astype(F32) + mix).astype(BF16)
        yield

    def proj_dots(half, left, n, place):
        def step(k, carry):
            yy, xx = place(k)
            par[yy, xx, tokens(half), :] = dot(left, wv[yy * SIDE + xx]).astype(BF16)
            return carry

        lax.fori_loop(0, n, step, 0)

    def add_to(ref, *others):
        total = ref[...].astype(F32)
        for o in others:
            total += o[...].astype(F32)
        ref[...] = total.astype(BF16)

    def sum_view(i):
        if GROUPS[i][1] == 0:
            return lambda j, p: par.at[j, :, piece(i, p), :]
        return lambda j, p: par.at[:, j, piece(i, p), :]

    early = {i: [] for i in range(len(GROUPS))}

    def landing(buf, p):
        return buf.at[:, pl.ds(*pieces[p]), :]

    def send_far(i):
        n, dev = ((y, y_dev), (x, x_dev))[GROUPS[i][1]]
        view = sum_view(i)
        near, other = bound(n)
        early[i].append(copy(view(ring(n, 2), 0), landing(buf1.at[i], 0), dev(other)))
        early[i].append(copy(view(ring(n, 2), 1), landing(buf1.at[i], 1), dev(near)))

    def send_near(i):
        n, dev = ((y, y_dev), (x, x_dev))[GROUPS[i][1]]
        view = sum_view(i)
        near, other = bound(n)
        early[i].append(copy(view(ring(n, near), 1), landing(buf2.at[i, 0], 1), dev(near)))
        early[i].append(copy(view(ring(n, other), 0), landing(buf2.at[i, 1], 0), dev(other)))

    def scatter(half):
        for c in w_copies:
            once(c)
        left = xs[SECTIONS, :, tokens(half)].T
        a, b = GROUPS.index((half, 0)), GROUPS.index((half, 1))
        proj_dots(half, left, 4, lambda k: (ring(y, 2), ring(x, k)))
        send_far(a)
        yield
        proj_dots(half, left, 3, lambda k: (ring(y, 3 + k), ring(x, 2)))
        send_far(b)
        yield
        proj_dots(
            half, left, 6,
            lambda k: (ring(y, 1 + 2 * lax.div(k, 3)), ring(x, 3 + lax.rem(k, 3))),
        )
        send_near(a)
        yield
        proj_dots(half, left, 3, lambda k: (y, ring(x, 3 + k)))
        send_near(b)
        yield

    def scatter_group(i):
        view, rows = sum_view(i), group(i)
        first = GROUPS[i][1]
        n, dev, dev2 = ((y, y_dev, x_dev), (x, x_dev, y_dev))[first]
        near, other = bound(n)
        a, b, c, d = early[i]
        a.wait_recv()
        add_to(view(ring(n, near), 0), landing(buf1.at[i], 0))
        e = copy(view(ring(n, near), 0), landing(buf2.at[i, 0], 0), dev(near))
        b.wait_recv()
        add_to(view(ring(n, other), 1), landing(buf1.at[i], 1))
        f = copy(view(ring(n, other), 1), landing(buf2.at[i, 1], 1), dev(other))
        yield
        c.wait_recv()
        f.wait_recv()
        add_to(view(n, 1), landing(buf2.at[i, 0], 1), landing(buf2.at[i, 1], 1))
        d.wait_recv()
        e.wait_recv()
        add_to(view(n, 0), landing(buf2.at[i, 0], 0), landing(buf2.at[i, 1], 0))
        copies = []
        for k in (2, 1, 3):
            src = par.at[y, ring(x, k), rows, :] if first == 0 else par.at[ring(y, k), x, rows, :]
            copies.append(copy(src, buf3.at[i, k - 1], dev2(k)))
        yield
        for c in copies:
            c.wait_recv()
        add_to(par.at[y, x, rows, :], *[buf3.at[i, k] for k in range(3)])
        copies = [
            copy(par.at[y, x, rows, columns(ring(z, k))], zr.at[i, k - 1], z_dev(k))
            for k in (1, 2, 3)
        ]
        yield
        total = par[y, x, rows, columns(z)].astype(F32)
        for k in (1, 2, 3):
            copies[k - 1].wait_recv()
            total += zr[i, k - 1].astype(F32)
        proj[rows, :] = total.astype(BF16)
        put(proj.at[rows, :], proj_out.at[rows, :])
        yield

    joined = []

    def backward(tiles, half):
        rows, cols = span(tiles), tokens(half)
        for s in reversed(range(SECTIONS)):
            c = copy(gs.at[s, rows, cols], gp.at[s, rows, cols], partner(s))
            if s not in joined:
                fac_copies[s].wait_recv()
                mp[s] = spread(fac_p[s])
                joined.append(s)
            yield
            c.wait_recv()
            for i in tiles:
                lo, w = TILES[i]
                own = gs[s, lo : lo + w, cols]
                back = dot(ma[s, 0:w, lo : lo + w], own)
                back += dot(mp[s, 0:w, lo : lo + w], gp[s, lo : lo + w, cols])
                new = (own.astype(F32) + back).astype(BF16)
                if s == 0:
                    hgrad[lo : lo + w, cols] = new
                else:
                    gs[s - 1, lo : lo + w, cols] = new
        put(hgrad.at[rows, cols], hgrad_out.at[rows, cols])
        yield

    keep = pl.ds(pl.multiple_of(HALF * core, HALF), HALF)
    give = pl.ds(pl.multiple_of(HALF - HALF * core, HALF), HALF)

    def factor(s):
        for act, rows in ((xs.at[s], own_rows(s)), (xp.at[s], other_rows(s))):
            for lo, w in TILES:
                full = dot(act[lo : lo + w, :], gs[s, lo : lo + w, :], NT)
                full = jnp.where(diag[:w, :w], full, 0.0)
                total = full[0:HALF]
                for g in range(1, w // HALF):
                    total += full[g * HALF : (g + 1) * HALF]
                fg[s, rows, lo : lo + w] = total
        yield

    def reduce(batch):
        some = pl.ds(min(batch), len(batch))
        if 0 in batch:
            a = copy(fg.at[some], fg_all.at[some], core_dev)
            yield
            a.wait_recv()
            chip = (fg[some] + fg_all[some]).astype(BF16)
            fg_half[some] = chip
            b = copy(fg_half.at[some, keep, :], fg_far.at[some, keep, :], far_dev)
            c = copy(fg_half.at[some, keep, :], fg_far.at[some, keep, :], cross_dev)
            yield
            b.wait_recv()
            c.wait_recv()
            total = chip.astype(F32) + fg_far[some].astype(F32)
        else:
            a = copy(fg.at[some, give, :], fg_core.at[some], core_dev)
            yield
            a.wait_recv()
            chip = (fg[some, keep, :] + fg_core[some]).astype(BF16)
            fg_half[some, keep, :] = chip
            b = copy(fg_half.at[some, keep, :], fg_far.at[some, keep, :], far_dev)
            yield
            b.wait_recv()
            fg_all[some, keep, :] = chip.astype(F32) + fg_far[some, keep, :].astype(F32)
            c = copy(fg_all.at[some, keep, :], fg_all.at[some, keep, :], core_dev)
            yield
            c.wait_recv()
            total = fg_all[some]
        total = total * (1.0 / (4 * ROWS))
        for j in range(LANES):
            fgrad[some, j] = total[:, :, 2 * HALF * j : 2 * HALF * (j + 1)]
        put(fgrad.at[some], fgrad_out.at[some])
        yield

    def greet():
        for r in range(3):
            for dev in ends:
                pl.semaphore_signal(word.at[r], inc=1, device_id=dev, device_id_type=MESH)
            yield
            pl.semaphore_wait(word.at[r], 2)
        pl.semaphore_signal(word.at[3], inc=1, device_id=core_dev, device_id_type=MESH)
        yield
        pl.semaphore_wait(word.at[3], 1)
        yield

    chains = {"S": setup(), "H": greet()}
    for half in range(HALVES):
        chains[f"N{half}"] = gather_dots(half)
        chains[f"R{half}"] = scatter(half)
    for i in range(len(GROUPS)):
        chains[f"G{i}"] = gather(i)
        chains[f"Q{i}"] = scatter_group(i)
    for i, part in enumerate(PARTS):
        chains[f"F{i}"] = forward(*part)
        chains[f"B{i}"] = backward(*part)
    for s in range(SECTIONS):
        chains[f"E{s}"] = factor(s)
    for i, batch in enumerate(BATCHES):
        chains[f"D{i}"] = reduce(batch)
    for name in sum(SCHEDULE, ()):
        next(chains[name], None)
    for chain in chains.values():
        for _ in chain:
            pass
    assert len(started) == COPIES
    for c in started:
        c.wait_send()
    for c in stored:
        c.wait()


COPIES = 6 + 12 * len(PARTS) + 24 * len(GROUPS) + 3 * len(BATCHES)
STORES = len(GROUPS) + len(PARTS) + len(BATCHES)


def hand_on(*refs):
    for i in range(3):
        refs[3 + i][...] = refs[i][...]


def body(hidden, weight, factors, cotangent):
    anywhere = pl.BlockSpec(memory_space=pl.ANY)
    groups, part = len(GROUPS), (SIDE, GROUP, BLOCK)
    acts = (SECTIONS, WIDTH, ROWS)
    scratch = [
        ((SIDE * SIDE, WIDTH, BLOCK), BF16),
        ((ROWS, COL), BF16),
        ((SECTIONS, LANES, 2 * HALF, 2 * HALF), BF16),
        ((SIDE, SIDE, ROWS, BLOCK), BF16),
        ((SIDE, SIDE, ROWS, BLOCK), BF16),
        ((SECTIONS + 1, WIDTH, ROWS), BF16),
        (acts, BF16),
        (acts, BF16),
        (acts, BF16),
        ((SECTIONS, 2 * HALF, WIDTH), BF16),
        ((SECTIONS, HALF, WIDTH), BF16),
        ((SECTIONS, COL, WIDTH), BF16),
        ((SECTIONS, WIDTH, COL), BF16),
        ((SECTIONS, WIDTH, COL), BF16),
        ((SECTIONS, COL, WIDTH), BF16),
        ((SECTIONS, 2 * HALF, WIDTH), F32),
        ((SECTIONS, HALF, WIDTH), F32),
        ((SECTIONS, 2 * HALF, WIDTH), BF16),
        ((SECTIONS, 2 * HALF, WIDTH), BF16),
        ((SECTIONS, 2 * HALF, WIDTH), F32),
        ((HALVES, WIDTH, TOKENS), F32),
        ((groups,) + part, BF16),
        ((groups, 2) + part, BF16),
        ((groups, 3, GROUP, BLOCK), BF16),
        ((groups, 3, GROUP, COL), BF16),
        ((ROWS, COL), BF16),
        ((WIDTH, ROWS), BF16),
        ((SECTIONS, LANES, 2 * HALF, 2 * HALF), F32),
    ]
    proj, hgrad, fgrad = pl.pallas_call(
        kernel,
        out_shape=(
            jax.ShapeDtypeStruct((ROWS, COL), BF16),
            jax.ShapeDtypeStruct((WIDTH, ROWS), BF16),
            jax.ShapeDtypeStruct((SECTIONS, LANES, 2 * HALF, 2 * HALF), F32),
        ),
        in_specs=[anywhere] * 4,
        out_specs=(anywhere,) * 3,
        scratch_shapes=[pltpu.VMEM(*one) for one in scratch]
        + [
            pltpu.SemaphoreType.DMA((3 + SIDE * SIDE,)),
            pltpu.SemaphoreType.DMA((STORES,)),
            pltpu.SemaphoreType.REGULAR((4,)),
            pltpu.SemaphoreType.DMA((COPIES,)),
            pltpu.SemaphoreType.DMA((COPIES,)),
        ],
        compiler_params=pltpu.CompilerParams(
            collective_id=0, has_side_effects=True, vmem_limit_bytes=56 * 1024 * 1024
        ),
        name="butterfly",
    )(hidden.T, weight, factors, cotangent)
    outs = (proj, hgrad, fgrad)
    proj, hgrad, fgrad = pl.pallas_call(
        hand_on,
        out_shape=tuple(jax.ShapeDtypeStruct(o.shape, o.dtype) for o in outs),
        in_specs=[pl.BlockSpec(memory_space=pltpu.VMEM)] * 3,
        out_specs=(pl.BlockSpec(memory_space=pltpu.VMEM),) * 3,
        name="hand_on",
    )(*outs)
    return proj, hgrad.T, fgrad


def solution(mesh):
    return jax.shard_map(
        body,
        mesh=mesh,
        in_specs=(
            P("dp", "tensor"),
            P("tensor", None),
            P(None, "tensor", None, None),
            P("dp", "tensor"),
        ),
        out_specs=(P("dp", "tensor"), P("dp", "tensor"), P(None, "tensor", None, None)),
        check_vma=False,
    )
```

```python
import jax
import jax.numpy as jnp
from jax import lax
from jax.experimental import pallas as pl
from jax.experimental.pallas import tpu as pltpu
from jax.sharding import PartitionSpec as P

MESH = pl.DeviceIdType.MESH
BF16 = jnp.bfloat16
F32 = jnp.float32

ROWS = 256
WIDTH = 448
LANES = 7
HALF = 32
SECTIONS = 6
SIDE = 4
COL = 128
BLOCK = SIDE * COL
HALVES = 2
TOKENS = ROWS // HALVES
GROUP = TOKENS // 2
SLACK = GROUP // 2
TILES = ((0, 128), (128, 128), (256, 128), (384, 64))
SPLIT = ((0, 1), (2, 3))
PARTS = tuple((tiles, half) for half in range(HALVES) for tiles in SPLIT)
GROUPS = tuple((half, first) for half in range(HALVES) for first in (0, 1))

BATCHES = ((5, 4, 3), (2, 1), (0,))

SCHEDULE = (
    ("G3", "G2", "G1", "F2", "G0", "S", "G3", "F1", "G2", "G1", "G0", "G3"),
    ("F1", "F0", "G2", "F3", "F0", "F1", "F3", "G3", "G2", "G0", "G3", "F1"),
    ("F0", "G2", "G1", "N1", "G2", "G3", "N1", "B3", "H", "F2", "B2", "G0"),
    ("F0", "F1", "G1", "B3", "F2", "G1", "F3", "G0", "B2", "H", "N0", "G0"),
    ("F0", "F1", "B3", "G1", "N0", "B1", "B2", "F2", "B0", "F0", "H", "F3"),
    ("B1", "B2", "B0", "F1", "B3", "F2", "F3", "F0", "B1", "R0", "B0", "H"),
    ("R0", "B2", "B3", "F3", "F2", "B1", "R0", "B0", "R0", "Q0", "E3", "E4"),
    ("H", "F3", "B2", "Q1", "B1", "F2", "R1", "R1", "B0", "R1", "R1", "B3"),
    ("E5", "D0", "B1", "Q2", "D0", "Q3", "B0", "E0", "D2", "Q1", "B1", "D2"),
    ("Q0", "B3", "E2", "E1", "D1", "Q2", "D1", "Q3", "B2", "D0", "Q1", "Q0"),
    ("Q2", "Q3", "D2", "D1", "Q1", "B0", "D0", "D1", "Q0", "Q2", "Q3"),
)


def dot(a, b, contract=((1,), (0,))):
    return lax.dot_general(a, b, (contract, ((), ())), preferred_element_type=F32)


NT = ((1,), (1,))


def kernel(
    hid, w_hbm, fac_hbm, cot_hbm, proj_out, hgrad_out, fgrad_out,
    wv, cotv, facv, cotg, par, xs, xp, gs, gp, fac_t, fac_p, ma, mat, mbt, mp,
    fg, fg_core, fg_half, fg_far, fg_all, acc, buf1, buf2, buf3, zr,
    proj, hgrad, fgrad, in_sem, out_sem, word, send, recv,
):
    dp = lax.axis_index("dp")
    t = lax.axis_index("tensor")
    y = lax.div(t, SIDE * SIDE)
    x = lax.rem(lax.div(t, SIDE), SIDE)
    z = lax.rem(t, SIDE)
    core = lax.rem(dp, 2)

    def ring(v, k):
        return lax.rem(v + k, SIDE)

    def at(yy, xx, zz):
        return (dp, (yy * SIDE + xx) * SIDE + zz)

    def y_dev(k):
        return at(ring(y, k), x, z)

    def x_dev(k):
        return at(y, ring(x, k), z)

    def z_dev(k):
        return at(y, x, ring(z, k))

    far = lax.rem(dp + 2, 4)
    core_dev = (dp + 1 - 2 * core, t)
    far_dev = (far, t)
    cross_dev = (far + 1 - 2 * core, t)

    def bit_of(s):
        return lax.rem(lax.div(t, 1 << s), 2)

    def partner(s):
        return (dp, t + (1 << s) * (1 - 2 * bit_of(s)))

    def own_rows(s):
        return pl.ds(pl.multiple_of(HALF * bit_of(s), HALF), HALF)

    def other_rows(s):
        return pl.ds(pl.multiple_of(HALF - HALF * bit_of(s), HALF), HALF)

    started = []

    def copy(src, dst, dev):
        k = len(started)
        c = pltpu.make_async_remote_copy(
            src_ref=src, dst_ref=dst, send_sem=send.at[k], recv_sem=recv.at[k],
            device_id=dev, device_id_type=MESH,
        )
        c.start()
        started.append(c)
        return c

    def fetch(src, dst, k):
        c = pltpu.make_async_copy(src, dst, in_sem.at[k])
        c.start()
        return c

    cot_copy = fetch(cot_hbm, cotv, 0)
    hid_copy = fetch(hid, xs.at[0], 1)
    fac_copy = fetch(fac_hbm, facv, 2)
    w_copies = [
        fetch(w_hbm.at[:, pl.ds(b * BLOCK, BLOCK)], wv.at[b], 3 + b) for b in range(SIDE * SIDE)
    ]
    stored = []

    def put(src, dst):
        c = pltpu.make_async_copy(src, dst, out_sem.at[len(stored)])
        c.start()
        stored.append(c)

    peers = [f(k) for f in (z_dev, x_dev, y_dev) for k in (1, 2, 3)]
    run = lax.div(dp, 2) * SIDE + z

    def run_dev(k):
        to = lax.rem(run + k, 2 * SIDE)
        return (lax.div(to, SIDE) * 2 + core, t - z + lax.rem(to, SIDE))

    ends = [run_dev(1), run_dev(2 * SIDE - 1)]
    peers += [core_dev] + ends
    barrier = pltpu.get_barrier_semaphore()
    for dev in peers:
        pl.semaphore_signal(barrier, inc=1, device_id=dev, device_id_type=MESH)
    diag = (
        lax.broadcasted_iota(jnp.int32, (COL, WIDTH), 0) // HALF
        == lax.rem(lax.broadcasted_iota(jnp.int32, (COL, WIDTH), 1), COL) // HALF
    )

    def spread(part):
        return jnp.where(diag, jnp.concatenate([part] * 4, axis=0), jnp.zeros((), BF16))

    def turned(ref, full):
        for lo, w in TILES:
            ref[lo : lo + w, 0:w] = full[0:w, lo : lo + w].T

    fac_copy.wait()
    for s in range(SECTIONS):
        fac_t[s] = jnp.concatenate([facv[s, j] for j in range(LANES)], axis=1)
        own = spread(fac_t[s, own_rows(s), :])
        ma[s] = own
        turned(mat.at[s], own)
        turned(mbt.at[s], spread(fac_t[s, other_rows(s), :]))
    cot_copy.wait()
    hid_copy.wait()
    pl.semaphore_wait(barrier, len(peers))

    def start_of(i):
        half, first = GROUPS[i]
        return TOKENS * half + GROUP * first

    def group(i):
        return pl.ds(start_of(i), GROUP)

    pieces = ((0, SLACK), (SLACK, GROUP - SLACK))

    def piece(i, p):
        return pl.ds(start_of(i) + pieces[p][0], pieces[p][1])

    def bound(v):
        return 1 + 2 * lax.rem(v, 2), 3 - 2 * lax.rem(v, 2)

    def tokens(half):
        return pl.ds(TOKENS * half, TOKENS)

    def gather_phase(view, i, dev):
        near, other = bound(i)
        r1 = copy(view(i, 0), view(i, 0), dev(near))
        l2 = copy(view(i, 1), view(i, 1), dev(other))
        r2 = copy(view(i, 1), view(i, 1), dev(near))
        l1 = copy(view(i, 0), view(i, 0), dev(other))
        yield
        r1.wait_recv()
        there = view(ring(i, near), 0)
        far1 = copy(there, there, dev(other))
        l2.wait_recv()
        there = view(ring(i, other), 1)
        far2 = copy(there, there, dev(near))
        yield
        r2.wait_recv()
        l1.wait_recv()
        yield
        far1.wait_recv()
        far2.wait_recv()
        yield

    def grad_dots(half, n, place):
        def step(k, carry):
            yy, xx = place(k)
            acc[half] += dot(wv[yy * SIDE + xx], cotg[yy, xx, tokens(half), :], NT)
            return carry

        lax.fori_loop(0, n, step, 0)

    def columns(zz):
        return pl.ds(pl.multiple_of(zz * COL, COL), COL)

    loaded = []

    def once(c):
        if all(c is not d for d in loaded):
            c.wait()
            loaded.append(c)

    def gather(i):
        first = GROUPS[i][1]
        dev, dev2, n = ((x_dev, y_dev, y), (y_dev, x_dev, x))[first]
        rows = group(i)
        mine = cotg.at[y, x, rows, columns(z)]
        copies = [copy(cotv.at[rows, :], mine, z_dev(k)) for k in (1, 2, 3)]
        mine[...] = cotv[rows, :]
        yield
        for c in copies:
            c.wait_recv()
        here = cotg.at[y, x, rows, :]
        copies = [copy(here, here, dev(k)) for k in (1, 3, 2)]
        yield
        for c in copies:
            c.wait_recv()
        if first == 0:
            yield from gather_phase(lambda j, p: cotg.at[j, :, piece(i, p), :], n, dev2)
        else:
            yield from gather_phase(lambda j, p: cotg.at[:, j, piece(i, p), :], n, dev2)

    def gather_dots(half):
        for c in w_copies:
            once(c)
        acc[half] = jnp.zeros((WIDTH, TOKENS), F32)
        grad_dots(half, 9, lambda k: (ring(y, 3 + lax.div(k, 3)), ring(x, 3 + lax.rem(k, 3))))
        yield
        grad_dots(
            half,
            7,
            lambda k: (
                ring(y, jnp.where(k < 4, 2, k - 1)),
                ring(x, jnp.where(k < 4, k, 2)),
            ),
        )
        gs[SECTIONS - 1, :, tokens(half)] = acc[half].astype(BF16)
        yield

    fac_copies = [None] * SECTIONS

    def setup():
        for s in reversed(range(SECTIONS)):
            fac_copies[s] = copy(fac_t.at[s, other_rows(s), :], fac_p.at[s], partner(s))
        yield

    def span(tiles):
        lo = TILES[tiles[0]][0]
        return pl.ds(lo, TILES[tiles[-1]][0] + TILES[tiles[-1]][1] - lo)

    def forward(tiles, half):
        rows, cols = span(tiles), tokens(half)
        for s in range(SECTIONS):
            c = copy(xs.at[s, rows, cols], xp.at[s, rows, cols], partner(s))
            yield
            c.wait_recv()
            for i in tiles:
                lo, w = TILES[i]
                own = xs[s, lo : lo + w, cols]
                mix = dot(mat[s, lo : lo + w, 0:w], own)
                mix += dot(mbt[s, lo : lo + w, 0:w], xp[s, lo : lo + w, cols])
                xs[s + 1, lo : lo + w, cols] = (own.astype(F32) + mix).astype(BF16)
        yield

    def proj_dots(half, left, n, place):
        def step(k, carry):
            yy, xx = place(k)
            par[yy, xx, tokens(half), :] = dot(left, wv[yy * SIDE + xx]).astype(BF16)
            return carry

        lax.fori_loop(0, n, step, 0)

    def add_to(ref, *others):
        total = ref[...].astype(F32)
        for o in others:
            total += o[...].astype(F32)
        ref[...] = total.astype(BF16)

    def sum_view(i):
        if GROUPS[i][1] == 0:
            return lambda j, p: par.at[j, :, piece(i, p), :]
        return lambda j, p: par.at[:, j, piece(i, p), :]

    early = {i: [] for i in range(len(GROUPS))}

    def landing(buf, p):
        return buf.at[:, pl.ds(*pieces[p]), :]

    def send_far(i):
        n, dev = ((y, y_dev), (x, x_dev))[GROUPS[i][1]]
        view = sum_view(i)
        near, other = bound(n)
        early[i].append(copy(view(ring(n, 2), 0), landing(buf1.at[i], 0), dev(other)))
        early[i].append(copy(view(ring(n, 2), 1), landing(buf1.at[i], 1), dev(near)))

    def send_near(i):
        n, dev = ((y, y_dev), (x, x_dev))[GROUPS[i][1]]
        view = sum_view(i)
        near, other = bound(n)
        early[i].append(copy(view(ring(n, near), 1), landing(buf2.at[i, 0], 1), dev(near)))
        early[i].append(copy(view(ring(n, other), 0), landing(buf2.at[i, 1], 0), dev(other)))

    def scatter(half):
        for c in w_copies:
            once(c)
        left = xs[SECTIONS, :, tokens(half)].T
        a, b = GROUPS.index((half, 0)), GROUPS.index((half, 1))
        proj_dots(half, left, 4, lambda k: (ring(y, 2), ring(x, k)))
        send_far(a)
        yield
        proj_dots(half, left, 3, lambda k: (ring(y, 3 + k), ring(x, 2)))
        send_far(b)
        yield
        proj_dots(
            half, left, 6,
            lambda k: (ring(y, 1 + 2 * lax.div(k, 3)), ring(x, 3 + lax.rem(k, 3))),
        )
        send_near(a)
        yield
        proj_dots(half, left, 3, lambda k: (y, ring(x, 3 + k)))
        send_near(b)
        yield

    def scatter_group(i):
        view, rows = sum_view(i), group(i)
        first = GROUPS[i][1]
        n, dev, dev2 = ((y, y_dev, x_dev), (x, x_dev, y_dev))[first]
        near, other = bound(n)
        a, b, c, d = early[i]
        a.wait_recv()
        add_to(view(ring(n, near), 0), landing(buf1.at[i], 0))
        e = copy(view(ring(n, near), 0), landing(buf2.at[i, 0], 0), dev(near))
        b.wait_recv()
        add_to(view(ring(n, other), 1), landing(buf1.at[i], 1))
        f = copy(view(ring(n, other), 1), landing(buf2.at[i, 1], 1), dev(other))
        yield
        c.wait_recv()
        f.wait_recv()
        add_to(view(n, 1), landing(buf2.at[i, 0], 1), landing(buf2.at[i, 1], 1))
        d.wait_recv()
        e.wait_recv()
        add_to(view(n, 0), landing(buf2.at[i, 0], 0), landing(buf2.at[i, 1], 0))
        copies = []
        for k in (2, 1, 3):
            src = par.at[y, ring(x, k), rows, :] if first == 0 else par.at[ring(y, k), x, rows, :]
            copies.append(copy(src, buf3.at[i, k - 1], dev2(k)))
        yield
        for c in copies:
            c.wait_recv()
        add_to(par.at[y, x, rows, :], *[buf3.at[i, k] for k in range(3)])
        copies = [
            copy(par.at[y, x, rows, columns(ring(z, k))], zr.at[i, k - 1], z_dev(k))
            for k in (1, 2, 3)
        ]
        yield
        total = par[y, x, rows, columns(z)].astype(F32)
        for k in (1, 2, 3):
            copies[k - 1].wait_recv()
            total += zr[i, k - 1].astype(F32)
        proj[rows, :] = total.astype(BF16)
        put(proj.at[rows, :], proj_out.at[rows, :])
        yield

    joined = []

    def backward(tiles, half):
        rows, cols = span(tiles), tokens(half)
        for s in reversed(range(SECTIONS)):
            c = copy(gs.at[s, rows, cols], gp.at[s, rows, cols], partner(s))
            if s not in joined:
                fac_copies[s].wait_recv()
                mp[s] = spread(fac_p[s])
                joined.append(s)
            yield
            c.wait_recv()
            for i in tiles:
                lo, w = TILES[i]
                own = gs[s, lo : lo + w, cols]
                back = dot(ma[s, 0:w, lo : lo + w], own)
                back += dot(mp[s, 0:w, lo : lo + w], gp[s, lo : lo + w, cols])
                new = (own.astype(F32) + back).astype(BF16)
                if s == 0:
                    hgrad[lo : lo + w, cols] = new
                else:
                    gs[s - 1, lo : lo + w, cols] = new
        put(hgrad.at[rows, cols], hgrad_out.at[rows, cols])
        yield

    keep = pl.ds(pl.multiple_of(HALF * core, HALF), HALF)
    give = pl.ds(pl.multiple_of(HALF - HALF * core, HALF), HALF)

    def factor(s):
        for act, rows in ((xs.at[s], own_rows(s)), (xp.at[s], other_rows(s))):
            for lo, w in TILES:
                full = dot(act[lo : lo + w, :], gs[s, lo : lo + w, :], NT)
                full = jnp.where(diag[:w, :w], full, 0.0)
                total = full[0:HALF]
                for g in range(1, w // HALF):
                    total += full[g * HALF : (g + 1) * HALF]
                fg[s, rows, lo : lo + w] = total
        yield

    def reduce(batch):
        some = pl.ds(min(batch), len(batch))
        if 0 in batch:
            a = copy(fg.at[some], fg_all.at[some], core_dev)
            yield
            a.wait_recv()
            chip = (fg[some] + fg_all[some]).astype(BF16)
            fg_half[some] = chip
            b = copy(fg_half.at[some, keep, :], fg_far.at[some, keep, :], far_dev)
            c = copy(fg_half.at[some, keep, :], fg_far.at[some, keep, :], cross_dev)
            yield
            b.wait_recv()
            c.wait_recv()
            total = chip.astype(F32) + fg_far[some].astype(F32)
        else:
            a = copy(fg.at[some, give, :], fg_core.at[some], core_dev)
            yield
            a.wait_recv()
            chip = (fg[some, keep, :] + fg_core[some]).astype(BF16)
            fg_half[some, keep, :] = chip
            b = copy(fg_half.at[some, keep, :], fg_far.at[some, keep, :], far_dev)
            yield
            b.wait_recv()
            fg_all[some, keep, :] = chip.astype(F32) + fg_far[some, keep, :].astype(F32)
            c = copy(fg_all.at[some, keep, :], fg_all.at[some, keep, :], core_dev)
            yield
            c.wait_recv()
            total = fg_all[some]
        total = total * (1.0 / (4 * ROWS))
        for j in range(LANES):
            fgrad[some, j] = total[:, :, 2 * HALF * j : 2 * HALF * (j + 1)]
        put(fgrad.at[some], fgrad_out.at[some])
        yield

    def greet():
        for r in range(3):
            for dev in ends:
                pl.semaphore_signal(word.at[r], inc=1, device_id=dev, device_id_type=MESH)
            yield
            pl.semaphore_wait(word.at[r], 2)
        pl.semaphore_signal(word.at[3], inc=1, device_id=core_dev, device_id_type=MESH)
        yield
        pl.semaphore_wait(word.at[3], 1)
        yield

    chains = {"S": setup(), "H": greet()}
    for half in range(HALVES):
        chains[f"N{half}"] = gather_dots(half)
        chains[f"R{half}"] = scatter(half)
    for i in range(len(GROUPS)):
        chains[f"G{i}"] = gather(i)
        chains[f"Q{i}"] = scatter_group(i)
    for i, part in enumerate(PARTS):
        chains[f"F{i}"] = forward(*part)
        chains[f"B{i}"] = backward(*part)
    for s in range(SECTIONS):
        chains[f"E{s}"] = factor(s)
    for i, batch in enumerate(BATCHES):
        chains[f"D{i}"] = reduce(batch)
    for name in sum(SCHEDULE, ()):
        next(chains[name], None)
    for chain in chains.values():
        for _ in chain:
            pass
    assert len(started) == COPIES
    for c in started:
        c.wait_send()
    for c in stored:
        c.wait()


COPIES = 6 + 12 * len(PARTS) + 24 * len(GROUPS) + 3 * len(BATCHES)
STORES = len(GROUPS) + len(PARTS) + len(BATCHES)


def hand_on(proj, hgrad, fgrad, proj_out, hgrad_out, fgrad_out, pv, hv, fv, in_sem, out_sem):
    moves = [(proj, pv, proj_out), (hgrad, hv, hgrad_out)]
    moves += [(fgrad.at[s], fv.at[s], fgrad_out.at[s]) for s in range(SECTIONS)]
    ins = [pltpu.make_async_copy(m[0], m[1], in_sem.at[i]) for i, m in enumerate(moves)]
    outs = [pltpu.make_async_copy(m[1], m[2], out_sem.at[i]) for i, m in enumerate(moves)]
    for c in ins:
        c.start()
    for i, o in zip(ins, outs):
        i.wait()
        o.start()
    for c in outs:
        c.wait()


def body(hidden, weight, factors, cotangent):
    anywhere = pl.BlockSpec(memory_space=pl.ANY)
    groups, part = len(GROUPS), (SIDE, GROUP, BLOCK)
    acts = (SECTIONS, WIDTH, ROWS)
    scratch = [
        ((SIDE * SIDE, WIDTH, BLOCK), BF16),
        ((ROWS, COL), BF16),
        ((SECTIONS, LANES, 2 * HALF, 2 * HALF), BF16),
        ((SIDE, SIDE, ROWS, BLOCK), BF16),
        ((SIDE, SIDE, ROWS, BLOCK), BF16),
        ((SECTIONS + 1, WIDTH, ROWS), BF16),
        (acts, BF16),
        (acts, BF16),
        (acts, BF16),
        ((SECTIONS, 2 * HALF, WIDTH), BF16),
        ((SECTIONS, HALF, WIDTH), BF16),
        ((SECTIONS, COL, WIDTH), BF16),
        ((SECTIONS, WIDTH, COL), BF16),
        ((SECTIONS, WIDTH, COL), BF16),
        ((SECTIONS, COL, WIDTH), BF16),
        ((SECTIONS, 2 * HALF, WIDTH), F32),
        ((SECTIONS, HALF, WIDTH), F32),
        ((SECTIONS, 2 * HALF, WIDTH), BF16),
        ((SECTIONS, 2 * HALF, WIDTH), BF16),
        ((SECTIONS, 2 * HALF, WIDTH), F32),
        ((HALVES, WIDTH, TOKENS), F32),
        ((groups,) + part, BF16),
        ((groups, 2) + part, BF16),
        ((groups, 3, GROUP, BLOCK), BF16),
        ((groups, 3, GROUP, COL), BF16),
        ((ROWS, COL), BF16),
        ((WIDTH, ROWS), BF16),
        ((SECTIONS, LANES, 2 * HALF, 2 * HALF), F32),
    ]
    proj, hgrad, fgrad = pl.pallas_call(
        kernel,
        out_shape=(
            jax.ShapeDtypeStruct((ROWS, COL), BF16),
            jax.ShapeDtypeStruct((WIDTH, ROWS), BF16),
            jax.ShapeDtypeStruct((SECTIONS, LANES, 2 * HALF, 2 * HALF), F32),
        ),
        in_specs=[anywhere] * 4,
        out_specs=(anywhere,) * 3,
        scratch_shapes=[pltpu.VMEM(*one) for one in scratch]
        + [
            pltpu.SemaphoreType.DMA((3 + SIDE * SIDE,)),
            pltpu.SemaphoreType.DMA((STORES,)),
            pltpu.SemaphoreType.REGULAR((4,)),
            pltpu.SemaphoreType.DMA((COPIES,)),
            pltpu.SemaphoreType.DMA((COPIES,)),
        ],
        compiler_params=pltpu.CompilerParams(
            collective_id=0, has_side_effects=True, vmem_limit_bytes=56 * 1024 * 1024
        ),
        name="butterfly",
    )(hidden.T, weight, factors, cotangent)
    outs = (proj, hgrad, fgrad)
    proj, hgrad, fgrad = pl.pallas_call(
        hand_on,
        out_shape=tuple(jax.ShapeDtypeStruct(o.shape, o.dtype) for o in outs),
        in_specs=[anywhere] * 3,
        out_specs=(anywhere,) * 3,
        scratch_shapes=[pltpu.VMEM(o.shape, o.dtype) for o in outs]
        + [pltpu.SemaphoreType.DMA((2 + SECTIONS,))] * 2,
        name="hand_on",
    )(*outs)
    return proj, hgrad.T, fgrad


def solution(mesh):
    return jax.shard_map(
        body,
        mesh=mesh,
        in_specs=(
            P("dp", "tensor"),
            P("tensor", None),
            P(None, "tensor", None, None),
            P("dp", "tensor"),
        ),
        out_specs=(P("dp", "tensor"), P("dp", "tensor"), P(None, "tensor", None, None)),
        check_vma=False,
    )
```

```python
import jax
import jax.numpy as jnp
from jax import lax
from jax.experimental import pallas as pl
from jax.experimental.pallas import tpu as pltpu
from jax.sharding import PartitionSpec as P

MESH = pl.DeviceIdType.MESH
BF16 = jnp.bfloat16
F32 = jnp.float32

ROWS = 256
WIDTH = 448
LANES = 7
HALF = 32
SECTIONS = 6
SIDE = 4
COL = 128
BLOCK = SIDE * COL
HALVES = 2
TOKENS = ROWS // HALVES
GROUP = TOKENS // 2
SLACK = GROUP // 2
TILES = ((0, 128), (128, 128), (256, 128), (384, 64))
SPLIT = ((0, 1), (2, 3))
PARTS = tuple((tiles, half) for half in range(HALVES) for tiles in SPLIT)
GROUPS = tuple((half, first) for half in range(HALVES) for first in (0, 1))

BATCHES = ((5, 4, 3), (2, 1), (0,))

SCHEDULE = (
    ("G3", "G2", "G1", "F2", "G0", "S", "G3", "F1", "G2", "G1", "G0", "G3"),
    ("F1", "F0", "G2", "F3", "F0", "F1", "F3", "G3", "G2", "G0", "G3", "F1"),
    ("F0", "G2", "G1", "N1", "G2", "G3", "N1", "B3", "H", "F2", "B2", "G0"),
    ("F0", "F1", "G1", "B3", "F2", "G1", "F3", "G0", "B2", "H", "N0", "G0"),
    ("F0", "F1", "B3", "G1", "N0", "B1", "B2", "F2", "B0", "F0", "H", "F3"),
    ("B1", "B2", "B0", "F1", "B3", "F2", "F3", "F0", "B1", "R0", "B0", "H"),
    ("R0", "B2", "B3", "F3", "F2", "B1", "R0", "B0", "R0", "Q0", "E3", "E4"),
    ("H", "F3", "B2", "Q1", "B1", "F2", "R1", "R1", "B0", "R1", "R1", "B3"),
    ("E5", "D0", "B1", "Q2", "D0", "Q3", "B0", "E0", "D2", "Q1", "B1", "D2"),
    ("Q0", "B3", "E2", "E1", "D1", "Q2", "D1", "Q3", "B2", "D0", "Q1", "Q0"),
    ("Q2", "Q3", "D2", "D1", "Q1", "B0", "D0", "D1", "Q0", "Q2", "Q3"),
)


def dot(a, b, contract=((1,), (0,))):
    return lax.dot_general(a, b, (contract, ((), ())), preferred_element_type=F32)


NT = ((1,), (1,))


def kernel(
    hid, w_hbm, fac_hbm, cot_hbm, proj_out, hgrad_out, fgrad_out,
    wv, cotv, facv, cotg, par, xs, xp, gs, gp, fac_t, fac_p, ma, mat, mbt, mp,
    fg, fg_core, fg_half, fg_far, fg_all, acc, buf1, buf2, buf3, zr,
    proj, hgrad, fgrad, in_sem, out_sem, word, send, recv,
):
    dp = lax.axis_index("dp")
    t = lax.axis_index("tensor")
    y = lax.div(t, SIDE * SIDE)
    x = lax.rem(lax.div(t, SIDE), SIDE)
    z = lax.rem(t, SIDE)
    core = lax.rem(dp, 2)

    def ring(v, k):
        return lax.rem(v + k, SIDE)

    def at(yy, xx, zz):
        return (dp, (yy * SIDE + xx) * SIDE + zz)

    def y_dev(k):
        return at(ring(y, k), x, z)

    def x_dev(k):
        return at(y, ring(x, k), z)

    def z_dev(k):
        return at(y, x, ring(z, k))

    far = lax.rem(dp + 2, 4)
    core_dev = (dp + 1 - 2 * core, t)
    far_dev = (far, t)
    cross_dev = (far + 1 - 2 * core, t)

    def bit_of(s):
        return lax.rem(lax.div(t, 1 << s), 2)

    def partner(s):
        return (dp, t + (1 << s) * (1 - 2 * bit_of(s)))

    def own_rows(s):
        return pl.ds(pl.multiple_of(HALF * bit_of(s), HALF), HALF)

    def other_rows(s):
        return pl.ds(pl.multiple_of(HALF - HALF * bit_of(s), HALF), HALF)

    started = []

    def copy(src, dst, dev):
        k = len(started)
        c = pltpu.make_async_remote_copy(
            src_ref=src, dst_ref=dst, send_sem=send.at[k], recv_sem=recv.at[k],
            device_id=dev, device_id_type=MESH,
        )
        c.start()
        started.append(c)
        return c

    peers = [f(k) for f in (z_dev, x_dev, y_dev) for k in (1, 2, 3)]
    run = lax.div(dp, 2) * SIDE + z

    def run_dev(k):
        to = lax.rem(run + k, 2 * SIDE)
        return (lax.div(to, SIDE) * 2 + core, t - z + lax.rem(to, SIDE))

    ends = [run_dev(1), run_dev(2 * SIDE - 1)]
    peers += [core_dev] + ends
    barrier = pltpu.get_barrier_semaphore()
    for dev in peers:
        pl.semaphore_signal(barrier, inc=1, device_id=dev, device_id_type=MESH)

    def fetch(src, dst, k):
        c = pltpu.make_async_copy(src, dst, in_sem.at[k])
        c.start()
        return c

    cot_copy = fetch(cot_hbm, cotv, 0)
    hid_copy = fetch(hid, xs.at[0], 1)
    fac_copy = fetch(fac_hbm, facv, 2)
    w_copies = [
        fetch(w_hbm.at[:, pl.ds(b * BLOCK, BLOCK)], wv.at[b], 3 + b) for b in range(SIDE * SIDE)
    ]
    stored = []

    def put(src, dst):
        c = pltpu.make_async_copy(src, dst, out_sem.at[len(stored)])
        c.start()
        stored.append(c)

    diag = (
        lax.broadcasted_iota(jnp.int32, (COL, WIDTH), 0) // HALF
        == lax.rem(lax.broadcasted_iota(jnp.int32, (COL, WIDTH), 1), COL) // HALF
    )

    def spread(part):
        return jnp.where(diag, jnp.concatenate([part] * 4, axis=0), jnp.zeros((), BF16))

    def turned(ref, full):
        for lo, w in TILES:
            ref[lo : lo + w, 0:w] = full[0:w, lo : lo + w].T

    fac_copy.wait()
    for s in range(SECTIONS):
        fac_t[s] = jnp.concatenate([facv[s, j] for j in range(LANES)], axis=1)
        own = spread(fac_t[s, own_rows(s), :])
        ma[s] = own
        turned(mat.at[s], own)
        turned(mbt.at[s], spread(fac_t[s, other_rows(s), :]))
    cot_copy.wait()
    hid_copy.wait()
    pl.semaphore_wait(barrier, len(peers))

    def start_of(i):
        half, first = GROUPS[i]
        return TOKENS * half + GROUP * first

    def group(i):
        return pl.ds(start_of(i), GROUP)

    pieces = ((0, SLACK), (SLACK, GROUP - SLACK))

    def piece(i, p):
        return pl.ds(start_of(i) + pieces[p][0], pieces[p][1])

    def bound(v):
        return 1 + 2 * lax.rem(v, 2), 3 - 2 * lax.rem(v, 2)

    def tokens(half):
        return pl.ds(TOKENS * half, TOKENS)

    def gather_phase(view, i, dev):
        near, other = bound(i)
        r1 = copy(view(i, 0), view(i, 0), dev(near))
        l2 = copy(view(i, 1), view(i, 1), dev(other))
        r2 = copy(view(i, 1), view(i, 1), dev(near))
        l1 = copy(view(i, 0), view(i, 0), dev(other))
        yield
        r1.wait_recv()
        there = view(ring(i, near), 0)
        far1 = copy(there, there, dev(other))
        l2.wait_recv()
        there = view(ring(i, other), 1)
        far2 = copy(there, there, dev(near))
        yield
        r2.wait_recv()
        l1.wait_recv()
        yield
        far1.wait_recv()
        far2.wait_recv()
        yield

    def grad_dots(half, n, place):
        def step(k, carry):
            yy, xx = place(k)
            acc[half] += dot(wv[yy * SIDE + xx], cotg[yy, xx, tokens(half), :], NT)
            return carry

        lax.fori_loop(0, n, step, 0)

    def columns(zz):
        return pl.ds(pl.multiple_of(zz * COL, COL), COL)

    loaded = []

    def once(c):
        if all(c is not d for d in loaded):
            c.wait()
            loaded.append(c)

    def gather(i):
        first = GROUPS[i][1]
        dev, dev2, n = ((x_dev, y_dev, y), (y_dev, x_dev, x))[first]
        rows = group(i)
        mine = cotg.at[y, x, rows, columns(z)]
        copies = [copy(cotv.at[rows, :], mine, z_dev(k)) for k in (1, 2, 3)]
        mine[...] = cotv[rows, :]
        yield
        for c in copies:
            c.wait_recv()
        here = cotg.at[y, x, rows, :]
        copies = [copy(here, here, dev(k)) for k in (1, 3, 2)]
        yield
        for c in copies:
            c.wait_recv()
        if first == 0:
            yield from gather_phase(lambda j, p: cotg.at[j, :, piece(i, p), :], n, dev2)
        else:
            yield from gather_phase(lambda j, p: cotg.at[:, j, piece(i, p), :], n, dev2)

    def gather_dots(half):
        for c in w_copies:
            once(c)
        acc[half] = jnp.zeros((WIDTH, TOKENS), F32)
        grad_dots(half, 9, lambda k: (ring(y, 3 + lax.div(k, 3)), ring(x, 3 + lax.rem(k, 3))))
        yield
        grad_dots(
            half,
            7,
            lambda k: (
                ring(y, jnp.where(k < 4, 2, k - 1)),
                ring(x, jnp.where(k < 4, k, 2)),
            ),
        )
        gs[SECTIONS - 1, :, tokens(half)] = acc[half].astype(BF16)
        yield

    fac_copies = [None] * SECTIONS

    def setup():
        for s in reversed(range(SECTIONS)):
            fac_copies[s] = copy(fac_t.at[s, other_rows(s), :], fac_p.at[s], partner(s))
        yield

    def span(tiles):
        lo = TILES[tiles[0]][0]
        return pl.ds(lo, TILES[tiles[-1]][0] + TILES[tiles[-1]][1] - lo)

    def forward(tiles, half):
        rows, cols = span(tiles), tokens(half)
        for s in range(SECTIONS):
            c = copy(xs.at[s, rows, cols], xp.at[s, rows, cols], partner(s))
            yield
            c.wait_recv()
            for i in tiles:
                lo, w = TILES[i]
                own = xs[s, lo : lo + w, cols]
                mix = dot(mat[s, lo : lo + w, 0:w], own)
                mix += dot(mbt[s, lo : lo + w, 0:w], xp[s, lo : lo + w, cols])
                xs[s + 1, lo : lo + w, cols] = (own.astype(F32) + mix).astype(BF16)
        yield

    def proj_dots(half, left, n, place):
        def step(k, carry):
            yy, xx = place(k)
            par[yy, xx, tokens(half), :] = dot(left, wv[yy * SIDE + xx]).astype(BF16)
            return carry

        lax.fori_loop(0, n, step, 0)

    def add_to(ref, *others):
        total = ref[...].astype(F32)
        for o in others:
            total += o[...].astype(F32)
        ref[...] = total.astype(BF16)

    def sum_view(i):
        if GROUPS[i][1] == 0:
            return lambda j, p: par.at[j, :, piece(i, p), :]
        return lambda j, p: par.at[:, j, piece(i, p), :]

    early = {i: [] for i in range(len(GROUPS))}

    def landing(buf, p):
        return buf.at[:, pl.ds(*pieces[p]), :]

    def send_far(i):
        n, dev = ((y, y_dev), (x, x_dev))[GROUPS[i][1]]
        view = sum_view(i)
        near, other = bound(n)
        early[i].append(copy(view(ring(n, 2), 0), landing(buf1.at[i], 0), dev(other)))
        early[i].append(copy(view(ring(n, 2), 1), landing(buf1.at[i], 1), dev(near)))

    def send_near(i):
        n, dev = ((y, y_dev), (x, x_dev))[GROUPS[i][1]]
        view = sum_view(i)
        near, other = bound(n)
        early[i].append(copy(view(ring(n, near), 1), landing(buf2.at[i, 0], 1), dev(near)))
        early[i].append(copy(view(ring(n, other), 0), landing(buf2.at[i, 1], 0), dev(other)))

    def scatter(half):
        for c in w_copies:
            once(c)
        left = xs[SECTIONS, :, tokens(half)].T
        a, b = GROUPS.index((half, 0)), GROUPS.index((half, 1))
        proj_dots(half, left, 4, lambda k: (ring(y, 2), ring(x, k)))
        send_far(a)
        yield
        proj_dots(half, left, 3, lambda k: (ring(y, 3 + k), ring(x, 2)))
        send_far(b)
        yield
        proj_dots(
            half, left, 6,
            lambda k: (ring(y, 1 + 2 * lax.div(k, 3)), ring(x, 3 + lax.rem(k, 3))),
        )
        send_near(a)
        yield
        proj_dots(half, left, 3, lambda k: (y, ring(x, 3 + k)))
        send_near(b)
        yield

    def scatter_group(i):
        view, rows = sum_view(i), group(i)
        first = GROUPS[i][1]
        n, dev, dev2 = ((y, y_dev, x_dev), (x, x_dev, y_dev))[first]
        near, other = bound(n)
        a, b, c, d = early[i]
        a.wait_recv()
        add_to(view(ring(n, near), 0), landing(buf1.at[i], 0))
        e = copy(view(ring(n, near), 0), landing(buf2.at[i, 0], 0), dev(near))
        b.wait_recv()
        add_to(view(ring(n, other), 1), landing(buf1.at[i], 1))
        f = copy(view(ring(n, other), 1), landing(buf2.at[i, 1], 1), dev(other))
        yield
        c.wait_recv()
        f.wait_recv()
        add_to(view(n, 1), landing(buf2.at[i, 0], 1), landing(buf2.at[i, 1], 1))
        d.wait_recv()
        e.wait_recv()
        add_to(view(n, 0), landing(buf2.at[i, 0], 0), landing(buf2.at[i, 1], 0))
        copies = []
        for k in (2, 1, 3):
            src = par.at[y, ring(x, k), rows, :] if first == 0 else par.at[ring(y, k), x, rows, :]
            copies.append(copy(src, buf3.at[i, k - 1], dev2(k)))
        yield
        for c in copies:
            c.wait_recv()
        add_to(par.at[y, x, rows, :], *[buf3.at[i, k] for k in range(3)])
        copies = [
            copy(par.at[y, x, rows, columns(ring(z, k))], zr.at[i, k - 1], z_dev(k))
            for k in (1, 2, 3)
        ]
        yield
        total = par[y, x, rows, columns(z)].astype(F32)
        for k in (1, 2, 3):
            copies[k - 1].wait_recv()
            total += zr[i, k - 1].astype(F32)
        proj[rows, :] = total.astype(BF16)
        put(proj.at[rows, :], proj_out.at[rows, :])
        yield

    joined = []

    def backward(tiles, half):
        rows, cols = span(tiles), tokens(half)
        for s in reversed(range(SECTIONS)):
            c = copy(gs.at[s, rows, cols], gp.at[s, rows, cols], partner(s))
            if s not in joined:
                fac_copies[s].wait_recv()
                mp[s] = spread(fac_p[s])
                joined.append(s)
            yield
            c.wait_recv()
            for i in tiles:
                lo, w = TILES[i]
                own = gs[s, lo : lo + w, cols]
                back = dot(ma[s, 0:w, lo : lo + w], own)
                back += dot(mp[s, 0:w, lo : lo + w], gp[s, lo : lo + w, cols])
                new = (own.astype(F32) + back).astype(BF16)
                if s == 0:
                    hgrad[lo : lo + w, cols] = new
                else:
                    gs[s - 1, lo : lo + w, cols] = new
        put(hgrad.at[rows, cols], hgrad_out.at[rows, cols])
        yield

    keep = pl.ds(pl.multiple_of(HALF * core, HALF), HALF)
    give = pl.ds(pl.multiple_of(HALF - HALF * core, HALF), HALF)

    def factor(s):
        for act, rows in ((xs.at[s], own_rows(s)), (xp.at[s], other_rows(s))):
            for lo, w in TILES:
                full = dot(act[lo : lo + w, :], gs[s, lo : lo + w, :], NT)
                full = jnp.where(diag[:w, :w], full, 0.0)
                total = full[0:HALF]
                for g in range(1, w // HALF):
                    total += full[g * HALF : (g + 1) * HALF]
                fg[s, rows, lo : lo + w] = total
        yield

    def reduce(batch):
        some = pl.ds(min(batch), len(batch))
        if 0 in batch:
            a = copy(fg.at[some], fg_all.at[some], core_dev)
            yield
            a.wait_recv()
            chip = (fg[some] + fg_all[some]).astype(BF16)
            fg_half[some] = chip
            b = copy(fg_half.at[some, keep, :], fg_far.at[some, keep, :], far_dev)
            c = copy(fg_half.at[some, keep, :], fg_far.at[some, keep, :], cross_dev)
            yield
            b.wait_recv()
            c.wait_recv()
            total = chip.astype(F32) + fg_far[some].astype(F32)
        else:
            a = copy(fg.at[some, give, :], fg_core.at[some], core_dev)
            yield
            a.wait_recv()
            chip = (fg[some, keep, :] + fg_core[some]).astype(BF16)
            fg_half[some, keep, :] = chip
            b = copy(fg_half.at[some, keep, :], fg_far.at[some, keep, :], far_dev)
            yield
            b.wait_recv()
            fg_all[some, keep, :] = chip.astype(F32) + fg_far[some, keep, :].astype(F32)
            c = copy(fg_all.at[some, keep, :], fg_all.at[some, keep, :], core_dev)
            yield
            c.wait_recv()
            total = fg_all[some]
        total = total * (1.0 / (4 * ROWS))
        for j in range(LANES):
            fgrad[some, j] = total[:, :, 2 * HALF * j : 2 * HALF * (j + 1)]
        put(fgrad.at[some], fgrad_out.at[some])
        yield

    def greet():
        for r in range(3):
            for dev in ends:
                pl.semaphore_signal(word.at[r], inc=1, device_id=dev, device_id_type=MESH)
            yield
            pl.semaphore_wait(word.at[r], 2)
        pl.semaphore_signal(word.at[3], inc=1, device_id=core_dev, device_id_type=MESH)
        yield
        pl.semaphore_wait(word.at[3], 1)
        yield

    chains = {"S": setup(), "H": greet()}
    for half in range(HALVES):
        chains[f"N{half}"] = gather_dots(half)
        chains[f"R{half}"] = scatter(half)
    for i in range(len(GROUPS)):
        chains[f"G{i}"] = gather(i)
        chains[f"Q{i}"] = scatter_group(i)
    for i, part in enumerate(PARTS):
        chains[f"F{i}"] = forward(*part)
        chains[f"B{i}"] = backward(*part)
    for s in range(SECTIONS):
        chains[f"E{s}"] = factor(s)
    for i, batch in enumerate(BATCHES):
        chains[f"D{i}"] = reduce(batch)
    for name in sum(SCHEDULE, ()):
        next(chains[name], None)
    for chain in chains.values():
        for _ in chain:
            pass
    assert len(started) == COPIES
    for c in started:
        c.wait_send()
    for c in stored:
        c.wait()


COPIES = 6 + 12 * len(PARTS) + 24 * len(GROUPS) + 3 * len(BATCHES)
STORES = len(GROUPS) + len(PARTS) + len(BATCHES)


def hand_on(proj, hgrad, fgrad, proj_out, hgrad_out, fgrad_out, pv, hv, fv, in_sem, out_sem):
    moves = [(proj, pv, proj_out), (hgrad, hv, hgrad_out)]
    moves += [(fgrad.at[s], fv.at[s], fgrad_out.at[s]) for s in range(SECTIONS)]
    ins = [pltpu.make_async_copy(m[0], m[1], in_sem.at[i]) for i, m in enumerate(moves)]
    outs = [pltpu.make_async_copy(m[1], m[2], out_sem.at[i]) for i, m in enumerate(moves)]
    for c in ins:
        c.start()
    for i, o in zip(ins, outs):
        i.wait()
        o.start()
    for c in outs:
        c.wait()


def body(hidden, weight, factors, cotangent):
    anywhere = pl.BlockSpec(memory_space=pl.ANY)
    groups, part = len(GROUPS), (SIDE, GROUP, BLOCK)
    acts = (SECTIONS, WIDTH, ROWS)
    scratch = [
        ((SIDE * SIDE, WIDTH, BLOCK), BF16),
        ((ROWS, COL), BF16),
        ((SECTIONS, LANES, 2 * HALF, 2 * HALF), BF16),
        ((SIDE, SIDE, ROWS, BLOCK), BF16),
        ((SIDE, SIDE, ROWS, BLOCK), BF16),
        ((SECTIONS + 1, WIDTH, ROWS), BF16),
        (acts, BF16),
        (acts, BF16),
        (acts, BF16),
        ((SECTIONS, 2 * HALF, WIDTH), BF16),
        ((SECTIONS, HALF, WIDTH), BF16),
        ((SECTIONS, COL, WIDTH), BF16),
        ((SECTIONS, WIDTH, COL), BF16),
        ((SECTIONS, WIDTH, COL), BF16),
        ((SECTIONS, COL, WIDTH), BF16),
        ((SECTIONS, 2 * HALF, WIDTH), F32),
        ((SECTIONS, HALF, WIDTH), F32),
        ((SECTIONS, 2 * HALF, WIDTH), BF16),
        ((SECTIONS, 2 * HALF, WIDTH), BF16),
        ((SECTIONS, 2 * HALF, WIDTH), F32),
        ((HALVES, WIDTH, TOKENS), F32),
        ((groups,) + part, BF16),
        ((groups, 2) + part, BF16),
        ((groups, 3, GROUP, BLOCK), BF16),
        ((groups, 3, GROUP, COL), BF16),
        ((ROWS, COL), BF16),
        ((WIDTH, ROWS), BF16),
        ((SECTIONS, LANES, 2 * HALF, 2 * HALF), F32),
    ]
    proj, hgrad, fgrad = pl.pallas_call(
        kernel,
        out_shape=(
            jax.ShapeDtypeStruct((ROWS, COL), BF16),
            jax.ShapeDtypeStruct((WIDTH, ROWS), BF16),
            jax.ShapeDtypeStruct((SECTIONS, LANES, 2 * HALF, 2 * HALF), F32),
        ),
        in_specs=[anywhere] * 4,
        out_specs=(anywhere,) * 3,
        scratch_shapes=[pltpu.VMEM(*one) for one in scratch]
        + [
            pltpu.SemaphoreType.DMA((3 + SIDE * SIDE,)),
            pltpu.SemaphoreType.DMA((STORES,)),
            pltpu.SemaphoreType.REGULAR((4,)),
            pltpu.SemaphoreType.DMA((COPIES,)),
            pltpu.SemaphoreType.DMA((COPIES,)),
        ],
        compiler_params=pltpu.CompilerParams(
            collective_id=0, has_side_effects=True, vmem_limit_bytes=56 * 1024 * 1024
        ),
        name="butterfly",
    )(hidden.T, weight, factors, cotangent)
    outs = (proj, hgrad, fgrad)
    proj, hgrad, fgrad = pl.pallas_call(
        hand_on,
        out_shape=tuple(jax.ShapeDtypeStruct(o.shape, o.dtype) for o in outs),
        in_specs=[anywhere] * 3,
        out_specs=(anywhere,) * 3,
        scratch_shapes=[pltpu.VMEM(o.shape, o.dtype) for o in outs]
        + [pltpu.SemaphoreType.DMA((2 + SECTIONS,))] * 2,
        name="hand_on",
    )(*outs)
    return proj, hgrad.T, fgrad


def solution(mesh):
    return jax.shard_map(
        body,
        mesh=mesh,
        in_specs=(
            P("dp", "tensor"),
            P("tensor", None),
            P(None, "tensor", None, None),
            P("dp", "tensor"),
        ),
        out_specs=(P("dp", "tensor"), P("dp", "tensor"), P(None, "tensor", None, None)),
        check_vma=False,
    )
```
